32 devices in a mesh: kv: 8 (over y, x, core), tp: 4 (over z).
Axes of the slice: x: 2, y: 2, z: 4, core: 2. Of those that a mesh axis runs over, the one named last changes fastest.
Arguments:
- activations: bfloat16 [64, 5120], P(('kv', 'tp')), may hold values from -27 to 27
- queries: bfloat16 [64, 5120], P('kv', 'tp'), may hold values from -16 to 16
- tree_cache_keys: bfloat16 [8192, 1024], P('kv', 'tp'), may hold values from -16 to 16
- tree_cache_values: bfloat16 [8192, 1024], P('kv', 'tp'), may hold values from -8 to 8
- parents: int32 [13], replicated, may hold values from 0 to 4, as said below
- node_lengths: int32 [13], replicated, may hold values from 1 to 2048, as said below
- token_leaf: int32 [64], replicated, may hold values from 5 to 12
- out_weight: bfloat16 [5120, 5120], P('tp'), may hold values from -0.078125 to 0.078125
- norm_gain: float32 [5120], replicated, may hold values from 0.5 to 1.5
- gate_weight: bfloat16 [5120, 27648], P(None, ('kv', 'tp')), may hold values from -0.078125 to 0.078125
- up_weight: bfloat16 [5120, 27648], P(None, ('kv', 'tp')), may hold values from -0.078125 to 0.078125
- down_weight: bfloat16 [27648, 5120], P(('kv', 'tp')), may hold values from -0.0390625 to 0.0390625
Outputs:
- output: bfloat16 [64, 5120], P(('kv', 'tp'))
The draws below stay inside these ranges and needn't reach their ends.
Inputs may be any that keep to these rules, and one draw needn't show every extreme that they name: Node 0 is the root, nodes 1 to 4 are tenants, the rest are leaves. parents[0] = 0, every tenant's parent is 0, every leaf's parent is a tenant, and every tenant is the parent of some leaf. `node_lengths`: the root holds exactly 2048 slots, every tenant at most 1024 and one tenant exactly that many, every leaf at most 256 and one leaf exactly that many. The nodes' slots follow one another in node order from slot 0.
All inputs are finite; a program needn't handle non-finite values.
Results may differ from the reference program's by a relative error of at most 0.017.
Values may be sent and summed in bfloat16 or wider, within the bound.
A program may use at most 128 MiB of HBM per device.

```python
import math
import jax
import jax.numpy as jnp
from jax import lax

D = 5120
QUERY_HEADS = 40
KEY_VALUE_HEADS = 8
HEAD_WIDTH = 128
FF = 27648
TENANTS = 4
TOKENS = 64
KEY_SLOTS = 8192
NODES = 13
NODE_MOST = 2048
LEAF_MOST = 256


def aligned_layout(key):
    sign_vector = jnp.sign(jax.random.normal(jax.random.fold_in(key, 4242), (HEAD_WIDTH,), jnp.float32))
    sign_vector = jnp.where(sign_vector == 0, 1.0, sign_vector)
    amplitude = math.sqrt(230.0 / math.sqrt(HEAD_WIDTH))
    return amplitude * sign_vector


def base_entry(key, shape):
    return jnp.clip(1.5 * jax.random.normal(key, shape, jnp.float32), -6.0, 6.0)


def draw_queries(key, part):
    values_entry = base_entry(jax.random.fold_in(key, 11), (TOKENS, QUERY_HEADS * HEAD_WIDTH))
    row_ids = jnp.arange(TOKENS)
    strength = 0.8 + 0.1 * (row_ids % 3).astype(jnp.float32)
    chosen = row_ids % 97 == 3
    layout = jnp.tile(aligned_layout(key), QUERY_HEADS)
    values_entry = jnp.where(chosen[:, None], strength[:, None] * layout[None, :], values_entry)
    return values_entry.astype(jnp.bfloat16)


def draw_tree_cache_keys(key, part):
    values_entry = base_entry(jax.random.fold_in(key, 12), (KEY_SLOTS, KEY_VALUE_HEADS * HEAD_WIDTH))
    row_ids = jnp.arange(KEY_SLOTS)
    layout = jnp.tile(aligned_layout(key), KEY_VALUE_HEADS)
    factor = jnp.where(row_ids == 0, 1.0, 0.99)
    values_entry = jnp.where((row_ids < 2)[:, None], factor[:, None] * layout[None, :], values_entry)
    return values_entry.astype(jnp.bfloat16)


def draw_activations(key, part):
    row_scale = jnp.exp(jax.random.uniform(jax.random.fold_in(key, 21), (TOKENS, 1), jnp.float32, math.log(0.3), math.log(3.0)))
    column_scale = jnp.exp(jax.random.uniform(jax.random.fold_in(key, 22), (1, D), jnp.float32, math.log(0.3), math.log(3.0)))
    values_entry = jnp.clip(jax.random.normal(jax.random.fold_in(key, 23), (TOKENS, D), jnp.float32), -3.0, 3.0)
    return (values_entry * row_scale * column_scale).astype(jnp.bfloat16)


def draw_parents(key, part):
    node_ids = jnp.arange(NODES, dtype=jnp.int32)
    picked = jax.random.randint(jax.random.fold_in(key, 31), (NODES,), 1, TENANTS + 1).astype(jnp.int32)
    leaf_rank = node_ids - 1 - TENANTS
    leaf_parent = jnp.where(leaf_rank < TENANTS, 1 + leaf_rank, picked)
    return jnp.where(node_ids <= TENANTS, 0, leaf_parent).astype(jnp.int32)


def draw_node_lengths(key, part):
    node_ids = jnp.arange(NODES, dtype=jnp.int32)
    tenant_sizes = jax.random.randint(jax.random.fold_in(key, 41), (NODES,), NODE_MOST // 8, NODE_MOST // 2 + 1).astype(jnp.int32)
    leaf_sizes = jax.random.randint(jax.random.fold_in(key, 42), (NODES,), 1, LEAF_MOST + 1).astype(jnp.int32)
    tenant_full = jax.random.randint(jax.random.fold_in(key, 43), (), 1, TENANTS + 1)
    leaf_full = jax.random.randint(jax.random.fold_in(key, 44), (), TENANTS + 1, NODES)
    tenant_sizes = jnp.where(node_ids == tenant_full, NODE_MOST // 2, tenant_sizes)
    leaf_sizes = jnp.where(node_ids == leaf_full, LEAF_MOST, leaf_sizes)
    return jnp.where(node_ids == 0, NODE_MOST, jnp.where(node_ids <= TENANTS, tenant_sizes, leaf_sizes)).astype(jnp.int32)


def place_ends(entries, own_key, smallest, largest):
    dims = entries.shape
    place = [jax.random.randint(jax.random.fold_in(own_key, axis), (), 0, dims[axis]) for axis in range(len(dims))]
    entries = entries.at[tuple(place)].set(smallest)
    longest = dims.index(max(dims))
    place[longest] = (place[longest] + 1) % dims[longest]
    return entries.at[tuple(place)].set(largest)


def level_of(rng, extent, split, least, high):
    gain, own = 1.0, jax.random.fold_in(rng, 6)
    for dim, blocks in split:
        draws = jnp.exp(jax.random.uniform(jax.random.fold_in(own, dim), (blocks,), jnp.float32, least / len(split), high / len(split)))
        gain = gain * jnp.repeat(draws, extent[dim] // blocks).reshape([-1 if axis == dim else 1 for axis in range(len(extent))])
    return gain


def centred(own_key, extent, spread, bound, pieces=(), held_as=jnp.bfloat16):
    array = jax.random.normal(own_key, extent, jnp.float32) * spread
    if len(pieces) > 0:
        array = level_of(own_key, extent, pieces, -0.22, 0.18) * array
    return jnp.clip(array, min=-bound, max=bound).astype(held_as)


def setup_inputs(seed: int = 0) -> dict:
    splits = jax.random.split(jax.random.key(seed), 13)
    activations = draw_activations(jax.random.fold_in(splits[12], 71), 0)
    queries = draw_queries(jax.random.fold_in(splits[12], 71), 0)
    tree_cache_keys = draw_tree_cache_keys(jax.random.fold_in(splits[12], 71), 0)
    tree_cache_values = centred(splits[3], (KEY_SLOTS, KEY_VALUE_HEADS * HEAD_WIDTH), 2.0, 8.0, ((0, 8), (1, 4)))
    parents = draw_parents(jax.random.fold_in(splits[12], 71), 0)
    node_lengths = draw_node_lengths(jax.random.fold_in(splits[12], 71), 0)
    token_leaf = place_ends(jax.random.randint(splits[6], (TOKENS,), TENANTS + 1, NODES), jax.random.fold_in(splits[6], 1), TENANTS + 1, NODES - 1).astype(jnp.int32)
    out_weight = centred(splits[7], (QUERY_HEADS * HEAD_WIDTH, D), (QUERY_HEADS * HEAD_WIDTH) ** -0.5, 0.078125, ((0, 4),))
    norm_gain = jnp.clip(1.0 + 0.1 * jax.random.normal(splits[8], (D,), jnp.float32), 0.5, 1.5)
    gate_weight = centred(splits[9], (D, FF), D ** -0.5, 0.078125, ((1, 32),))
    up_weight = centred(splits[10], (D, FF), D ** -0.5, 0.078125, ((1, 32),))
    down_weight = centred(splits[11], (FF, D), FF ** -0.5, 0.0390625, ((0, 32),))
    return {"activations": activations, "queries": queries, "tree_cache_keys": tree_cache_keys, "tree_cache_values": tree_cache_values, "parents": parents, "node_lengths": node_lengths, "token_leaf": token_leaf, "out_weight": out_weight, "norm_gain": norm_gain, "gate_weight": gate_weight, "up_weight": up_weight, "down_weight": down_weight}


LOWEST = -1e+30
EPSILON = 1e-06

def slot_owner(node_lengths, slot_total):
    node_ends = jnp.cumsum(node_lengths).astype(jnp.int32)
    node_starts = (node_ends - node_lengths).astype(jnp.int32)
    slot_ids = jnp.arange(slot_total, dtype=jnp.int32)
    inside = (slot_ids[:, None] >= node_starts[None, :]) & (slot_ids[:, None] < node_ends[None, :])
    labels = jnp.arange(node_lengths.shape[0], dtype=jnp.int32)
    holder = lax.optimization_barrier(jnp.sum(jnp.where(inside, labels[None, :], 0), axis=1)).astype(jnp.int32)
    return jnp.where(jnp.any(inside, axis=1), holder, -1).astype(jnp.int32)

def parent_of(node_ids, parents):
    labels = jnp.arange(parents.shape[0], dtype=jnp.int32)
    return lax.optimization_barrier(jnp.sum(jnp.where(node_ids[:, None] == labels[None, :], parents[None, :], 0), axis=1)).astype(jnp.int32)

def reference(activations, queries, tree_cache_keys, tree_cache_values, parents, node_lengths, token_leaf, out_weight, norm_gain, gate_weight, up_weight, down_weight):
    heads_per_group = QUERY_HEADS // KEY_VALUE_HEADS
    slot_node = slot_owner(node_lengths, KEY_SLOTS)
    tenant = parent_of(token_leaf, parents)
    block_length = math.gcd(TOKENS, 128)
    count_of_blocks = TOKENS // block_length
    score_scale = 1.0 / math.sqrt(HEAD_WIDTH)
    query_head_rows = queries.reshape(count_of_blocks, block_length, KEY_VALUE_HEADS, heads_per_group, HEAD_WIDTH).transpose(2, 0, 1, 3, 4)
    key_head_rows = tree_cache_keys.reshape(KEY_SLOTS, KEY_VALUE_HEADS, HEAD_WIDTH).transpose(1, 0, 2)
    value_head_rows = tree_cache_values.reshape(KEY_SLOTS, KEY_VALUE_HEADS, HEAD_WIDTH).transpose(1, 0, 2)
    leaf_blocks = token_leaf.reshape(count_of_blocks, block_length)
    tenant_blocks = tenant.reshape(count_of_blocks, block_length)

    def one_head(packed):
        query_head, key_rows, value_rows = packed
        keys_wide = key_rows.astype(jnp.float32)
        values_wide = value_rows.astype(jnp.float32)

        def one_block(blocked):
            query_block, leaf_ids, tenant_ids = blocked
            scores = jnp.einsum('tgd,sd->tgs', query_block.astype(jnp.float32), keys_wide) * score_scale
            allowed = (slot_node[None, :] == 0) | (slot_node[None, :] == tenant_ids[:, None]) | (slot_node[None, :] == leaf_ids[:, None])
            allowed = allowed[:, None, :]
            highest = lax.optimization_barrier(jnp.max(jnp.where(allowed, scores, LOWEST), axis=2, keepdims=True))
            weights = jnp.exp(jnp.where(allowed, scores - highest, -jnp.inf))
            denominator = lax.optimization_barrier(jnp.sum(weights, axis=2))
            rounded = lax.optimization_barrier(weights.astype(jnp.bfloat16)).astype(jnp.float32)
            weighted = jnp.einsum('tgs,sd->tgd', rounded, values_wide)
            return (weighted / denominator[..., None]).astype(jnp.bfloat16)
        return lax.map(one_block, (query_head, leaf_blocks, tenant_blocks))
    context = lax.map(one_head, (query_head_rows, key_head_rows, value_head_rows))
    context = context.transpose(1, 2, 0, 3, 4).reshape(TOKENS, QUERY_HEADS * HEAD_WIDTH)
    attended = jnp.dot(context, out_weight, preferred_element_type=jnp.float32)
    residual = (activations.astype(jnp.float32) + attended).astype(jnp.bfloat16)
    widened = residual.astype(jnp.float32)
    normed = (widened * lax.rsqrt(lax.optimization_barrier(jnp.mean(widened * widened, axis=1, keepdims=True)) + EPSILON) * norm_gain).astype(jnp.bfloat16)
    gate_proj = jnp.dot(normed, gate_weight, preferred_element_type=jnp.float32)
    up_proj = jnp.dot(normed, up_weight, preferred_element_type=jnp.float32)
    hidden = (jax.nn.silu(gate_proj) * up_proj).astype(jnp.bfloat16)
    down_proj = jnp.dot(hidden, down_weight, preferred_element_type=jnp.float32)
    return (widened + down_proj).astype(jnp.bfloat16)
```

```python
import functools
import math

import jax
import jax.numpy as jnp
from jax import lax
from jax.experimental import pallas as pl
from jax.experimental.pallas import tpu as pltpu
from jax.sharding import PartitionSpec as P

QUERY_HEADS = 40
KEY_VALUE_HEADS = 8
HEAD_WIDTH = 128
LOWEST = -1e30
EPSILON = 1e-06
MESH = pl.DeviceIdType.MESH
F32 = jnp.float32
BF16 = jnp.bfloat16


def copy_to(source, target, send, receive, axis, peer):
    return pltpu.make_async_remote_copy(
        src_ref=source,
        dst_ref=target,
        send_sem=send,
        recv_sem=receive,
        device_id={axis: peer},
        device_id_type=MESH,
    )


def layer_kernel(
    nk,
    nt,
    parts,
    parents,
    lengths,
    leaf_row,
    act,
    query,
    gain,
    keys_hbm,
    values_hbm,
    out_hbm,
    gate_hbm,
    up_hbm,
    down_hbm,
    result,
    keys,
    values,
    out_w,
    gate_w,
    up_w,
    down_w,
    q_all,
    act_all,
    w_send,
    w_recv,
    ml_send,
    ml_recv,
    p_send,
    p_recv,
    res,
    normed,
    acc_gate,
    acc_up,
    s_send,
    s_recv,
    f_send,
    f_recv,
    own,
    load_sem,
    q_ss,
    q_rs,
    a_ss,
    a_rs,
    w_ss,
    w_rs,
    ml_ss,
    ml_rs,
    p_ss,
    p_rs,
    rt_ss,
    rt_rs,
    rk_ss,
    rk_rs,
    s_ss,
    s_rs,
    f_ss,
    f_rs,
):
    k_me = lax.axis_index("kv")
    t_me = lax.axis_index("tp")
    group, q_width = query.shape
    tokens = nk * group
    slots = keys.shape[0]
    kv_local = keys.shape[1] // HEAD_WIDTH
    per_kv = QUERY_HEADS // KEY_VALUE_HEADS
    width = act.shape[1]
    rows_own = act.shape[0]
    cols = width // nt

    loads = [
        pltpu.make_async_copy(source, target, load_sem.at[i])
        for i, (source, target) in enumerate(
            (
                (keys_hbm, keys),
                (values_hbm, values),
                (out_hbm, out_w),
                (gate_hbm, gate_w),
                (up_hbm, up_w),
                (down_hbm, down_w),
            )
        )
    ]
    for load in loads:
        load.start()

    q_all[k_me] = query[...]
    act_all[t_me] = act[...].astype(F32)

    barrier = pltpu.get_barrier_semaphore()
    for d in range(1, nk):
        pl.semaphore_signal(
            barrier, inc=1, device_id={"kv": lax.rem(k_me + d, nk)}, device_id_type=MESH
        )
    for d in range(1, nt):
        pl.semaphore_signal(
            barrier, inc=1, device_id={"tp": lax.rem(t_me + d, nt)}, device_id_type=MESH
        )
    pl.semaphore_wait(barrier, nk + nt - 2)

    kv_to = [lax.rem(k_me + d, nk) for d in range(nk)]
    kv_from = [lax.rem(k_me + nk - d, nk) for d in range(nk)]
    tp_to = [lax.rem(t_me + d, nt) for d in range(nt)]
    tp_from = [lax.rem(t_me + nt - d, nt) for d in range(nt)]
    sends = []

    def send(*args):
        copy = copy_to(*args)
        copy.start()
        sends.append(copy)

    for d in range(1, nk):
        send(q_all.at[k_me], q_all.at[k_me], q_ss.at[d], q_rs.at[d], "kv", kv_to[d])
    for d in range(1, nt):
        send(act_all.at[t_me], act_all.at[t_me], a_ss.at[d], a_rs.at[d], "tp", tp_to[d])

    slot_id = k_me * slots + lax.broadcasted_iota(jnp.int32, (1, slots), 1)
    node = jnp.zeros((1, slots), jnp.int32)
    end = jnp.int32(0)
    nodes = parents.shape[0]
    for n in range(nodes):
        end = end + lengths[n]
        node = node + jnp.where(slot_id >= end, 1, 0)
    node = jnp.where(node == nodes, -1, node)
    diagonal = lax.broadcasted_iota(jnp.int32, (tokens, tokens), 0) == lax.broadcasted_iota(
        jnp.int32, (tokens, tokens), 1
    )
    leaf = jnp.sum(
        jnp.where(diagonal, jnp.broadcast_to(leaf_row[...], (tokens, tokens)), 0),
        axis=1,
        keepdims=True,
    )
    tenant = jnp.zeros_like(leaf)
    for n in range(nodes):
        tenant = tenant + jnp.where(leaf == n, parents[n], 0)
    allowed = ((node == 0) | (node == tenant) | (node == leaf))[None]

    loads[0].wait()
    loads[1].wait()
    for d in range(1, nk):
        block = q_all.at[kv_from[d]]
        copy_to(block, block, q_ss.at[d], q_rs.at[d], "kv", kv_to[d]).wait_recv()

    lane = lax.broadcasted_iota(jnp.int32, (tokens, HEAD_WIDTH), 1)
    tops = jnp.zeros((tokens, HEAD_WIDTH), F32)
    sums = jnp.ones((tokens, HEAD_WIDTH), F32)
    for j in range(kv_local):
        stacked = jnp.concatenate(
            [
                q_all[:, :, h * HEAD_WIDTH : (h + 1) * HEAD_WIDTH]
                .astype(F32)
                .reshape(tokens, HEAD_WIDTH)
                for h in range(j * per_kv, (j + 1) * per_kv)
            ],
            axis=0,
        ).astype(BF16)
        head = slice(j * HEAD_WIDTH, (j + 1) * HEAD_WIDTH)
        scores = lax.dot_general(
            stacked, keys[:, head], (((1,), (1,)), ((), ())), preferred_element_type=F32
        ) * (1.0 / math.sqrt(HEAD_WIDTH))
        scores = scores.reshape(per_kv, tokens, slots)
        top = jnp.max(jnp.where(allowed, scores, LOWEST), axis=2, keepdims=True)
        weights = jnp.where(allowed, jnp.exp(jnp.minimum(scores - top, 0.0)), 0.0)
        total = jnp.sum(weights, axis=2, keepdims=True)
        weighted = jnp.dot(
            weights.astype(BF16).reshape(per_kv * tokens, slots),
            values[:, head],
            preferred_element_type=F32,
        ).reshape(per_kv, nk, group, HEAD_WIDTH)
        for g in range(per_kv):
            h = j * per_kv + g
            w_send[:, :, h * HEAD_WIDTH : (h + 1) * HEAD_WIDTH] = weighted[g].astype(BF16)
            tops = jnp.where(lane == h, top[g], tops)
            sums = jnp.where(lane == h, total[g], sums)
    ml_send[:, 0] = tops.reshape(nk, group, HEAD_WIDTH)
    ml_send[:, 1] = sums.reshape(nk, group, HEAD_WIDTH)

    for d in range(1, nk):
        send(ml_send.at[kv_to[d]], ml_recv.at[d], ml_ss.at[d], ml_rs.at[d], "kv", kv_to[d])
        send(w_send.at[kv_to[d]], w_recv.at[d], w_ss.at[d], w_rs.at[d], "kv", kv_to[d])
    ml_recv[0] = ml_send[k_me]
    w_recv[0] = w_send[k_me]
    loads[2].wait()
    for d in range(1, nk):
        copy_to(
            ml_send.at[kv_to[d]], ml_recv.at[d], ml_ss.at[d], ml_rs.at[d], "kv", kv_to[d]
        ).wait_recv()
        copy_to(
            w_send.at[kv_to[d]], w_recv.at[d], w_ss.at[d], w_rs.at[d], "kv", kv_to[d]
        ).wait_recv()
    highest = ml_recv[0, 0]
    for d in range(1, nk):
        highest = jnp.maximum(highest, ml_recv[d, 0])
    scales = [jnp.exp(ml_recv[d, 0] - highest) for d in range(nk)]
    denominator = scales[0] * ml_recv[0, 1]
    for d in range(1, nk):
        denominator = denominator + scales[d] * ml_recv[d, 1]
    pieces = []
    for h in range(kv_local * per_kv):
        total = jnp.zeros((group, HEAD_WIDTH), F32)
        for d in range(nk):
            part = w_recv[d, :, h * HEAD_WIDTH : (h + 1) * HEAD_WIDTH].astype(F32)
            total = total + part * scales[d][:, h : h + 1]
        pieces.append(total / denominator[:, h : h + 1])
    context = jnp.concatenate(pieces, axis=1).astype(BF16)

    for d in list(range(1, nt)) + [0]:
        at = pl.multiple_of(tp_to[d] * cols, 128)
        product = jnp.dot(context, out_w[:, pl.ds(at, cols)], preferred_element_type=F32)
        if d > 0:
            p_send[d] = product.astype(BF16)
            send(p_send.at[d], p_recv.at[d], p_ss.at[d], p_rs.at[d], "tp", tp_to[d])
    for d in range(1, nt):
        block = act_all.at[tp_from[d]]
        copy_to(block, block, a_ss.at[d], a_rs.at[d], "tp", tp_to[d]).wait_recv()
    mine = pl.ds(pl.multiple_of(t_me * cols, 128), cols)
    row = lax.broadcasted_iota(jnp.int32, (group, cols), 0)
    before = jnp.zeros((group, cols), F32)
    for t in range(nt):
        block = act_all[t, :, mine]
        for i in range(rows_own):
            before = jnp.where(
                row == t * rows_own + i, jnp.broadcast_to(block[i : i + 1], (group, cols)), before
            )
    attended = product
    for d in range(1, nt):
        copy_to(
            p_send.at[d], p_recv.at[d], p_ss.at[d], p_rs.at[d], "tp", tp_to[d]
        ).wait_recv()
        attended = attended + p_recv[d].astype(F32)
    res[k_me, t_me] = (before + attended).astype(BF16)

    for d in range(1, nt):
        block = res.at[k_me, t_me]
        send(block, block, rt_ss.at[d], rt_rs.at[d], "tp", tp_to[d])
    for d in range(1, nt):
        block = res.at[k_me, tp_from[d]]
        copy_to(block, block, rt_ss.at[d], rt_rs.at[d], "tp", tp_to[d]).wait_recv()
    for d in range(1, nk):
        send(res.at[k_me], res.at[k_me], rk_ss.at[d], rk_rs.at[d], "kv", kv_to[d])
    loads[3].wait()
    loads[4].wait()
    loads[5].wait()
    acc_gate[...] = jnp.zeros_like(acc_gate)
    acc_up[...] = jnp.zeros_like(acc_up)
    for d in range(1, nk):
        block = res.at[kv_from[d]]
        copy_to(block, block, rk_ss.at[d], rk_rs.at[d], "kv", kv_to[d]).wait_recv()

    for p in range(nk // 2):
        pair = [
            res[2 * p : 2 * p + 2, c].astype(F32).reshape(2 * group, cols) for c in range(nt)
        ]
        square = sum(jnp.sum(part * part, axis=1, keepdims=True) for part in pair)
        inverse = lax.rsqrt(square / width + EPSILON)
        for c in range(nt):
            at = slice(c * cols, (c + 1) * cols)
            normed[2 * p * group : 2 * (p + 1) * group, at] = (
                pair[c] * inverse * gain[:, at]
            ).astype(BF16)

    step = 640

    @pl.loop(0, width // step)
    def _(i):
        at = pl.ds(pl.multiple_of(i * step, 128), step)
        x = normed[:, at]
        acc_gate[...] += jnp.dot(x, gate_w[at, :], preferred_element_type=F32)
        acc_up[...] += jnp.dot(x, up_w[at, :], preferred_element_type=F32)

    gate = acc_gate[...]
    hidden = (gate / (1.0 + jnp.exp(-gate)) * acc_up[...]).astype(BF16)

    chunk = width // parts
    for c in range(parts):
        at = slice(c * chunk, (c + 1) * chunk)
        product = jnp.dot(hidden, down_w[:, at], preferred_element_type=F32)
        s_send[c] = product.reshape(nk, group, chunk).astype(BF16)
        for d in range(1, nk):
            send(
                s_send.at[c, kv_to[d]],
                s_recv.at[c, d],
                s_ss.at[c, d],
                s_rs.at[c, d],
                "kv",
                kv_to[d],
            )

    row = lax.broadcasted_iota(jnp.int32, (group, cols), 0)
    for c in range(parts):
        at = slice(c * chunk, (c + 1) * chunk)
        mixed = s_send[c, k_me].astype(F32)
        for d in range(1, nk):
            copy_to(
                s_send.at[c, kv_to[d]],
                s_recv.at[c, d],
                s_ss.at[c, d],
                s_rs.at[c, d],
                "kv",
                kv_to[d],
            ).wait_recv()
            mixed = mixed + s_recv[c, d].astype(F32)
        for t in range(nt):
            f_send[c, t] = mixed[t * rows_own : (t + 1) * rows_own].astype(BF16)
        for d in range(1, nt):
            send(
                f_send.at[c, tp_to[d]],
                f_recv.at[c, d],
                f_ss.at[c, d],
                f_rs.at[c, d],
                "tp",
                tp_to[d],
            )
        for b in range(chunk // cols):
            first = c * (chunk // cols) + b
            here = mixed[:, b * cols : (b + 1) * cols] + res[k_me, first].astype(F32)
            for i in range(rows_own):
                own[i : i + 1, first * cols : (first + 1) * cols] = jnp.sum(
                    jnp.where(row == t_me * rows_own + i, here, 0.0), axis=0, keepdims=True
                )
    for c in range(parts):
        at = slice(c * chunk, (c + 1) * chunk)
        total = own[:, at]
        for d in range(1, nt):
            copy_to(
                f_send.at[c, tp_to[d]],
                f_recv.at[c, d],
                f_ss.at[c, d],
                f_rs.at[c, d],
                "tp",
                tp_to[d],
            ).wait_recv()
            total = total + f_recv[c, d].astype(F32)
        result[:, at] = total.astype(BF16)
    for copy in sends:
        copy.wait_send()


def local(
    nk,
    nt,
    activations,
    queries,
    tree_cache_keys,
    tree_cache_values,
    parents,
    node_lengths,
    token_leaf,
    out_weight,
    norm_gain,
    gate_weight,
    up_weight,
    down_weight,
):
    group, q_width = queries.shape
    rows_own, width = activations.shape
    tokens = nk * group
    cols = width // nt
    units = gate_weight.shape[1]
    parts = 2
    chunk = width // parts
    dma = pltpu.SemaphoreType.DMA
    vmem = pl.BlockSpec(memory_space=pltpu.VMEM)
    smem = pl.BlockSpec(memory_space=pltpu.SMEM)
    anywhere = pl.BlockSpec(memory_space=pl.ANY)
    return pl.pallas_call(
        functools.partial(layer_kernel, nk, nt, parts),
        out_shape=jax.ShapeDtypeStruct((rows_own, width), BF16),
        in_specs=[smem, smem, vmem, vmem, vmem, vmem] + [anywhere] * 6,
        out_specs=vmem,
        scratch_shapes=[
            pltpu.VMEM(tree_cache_keys.shape, BF16),
            pltpu.VMEM(tree_cache_values.shape, BF16),
            pltpu.VMEM(out_weight.shape, BF16),
            pltpu.VMEM(gate_weight.shape, BF16),
            pltpu.VMEM(up_weight.shape, BF16),
            pltpu.VMEM(down_weight.shape, BF16),
            pltpu.VMEM((nk, group, q_width), BF16),
            pltpu.VMEM((nt, rows_own, width), F32),
            pltpu.VMEM((nk, group, q_width), BF16),
            pltpu.VMEM((nk, group, q_width), BF16),
            pltpu.VMEM((nk, 2, group, HEAD_WIDTH), F32),
            pltpu.VMEM((nk, 2, group, HEAD_WIDTH), F32),
            pltpu.VMEM((nt, group, cols), BF16),
            pltpu.VMEM((nt, group, cols), BF16),
            pltpu.VMEM((nk, nt, group, cols), BF16),
            pltpu.VMEM((tokens, width), BF16),
            pltpu.VMEM((tokens, units), F32),
            pltpu.VMEM((tokens, units), F32),
            pltpu.VMEM((parts, nk, group, chunk), BF16),
            pltpu.VMEM((parts, nk, group, chunk), BF16),
            pltpu.VMEM((parts, nt, rows_own, chunk), BF16),
            pltpu.VMEM((parts, nt, rows_own, chunk), BF16),
            pltpu.VMEM((rows_own, width), F32),
            dma((6,)),
            dma((nk,)),
            dma((nk,)),
            dma((nt,)),
            dma((nt,)),
            dma((nk,)),
            dma((nk,)),
            dma((nk,)),
            dma((nk,)),
            dma((nt,)),
            dma((nt,)),
            dma((nt,)),
            dma((nt,)),
            dma((nk,)),
            dma((nk,)),
            dma((parts, nk)),
            dma((parts, nk)),
            dma((parts, nt)),
            dma((parts, nt)),
        ],
        compiler_params=pltpu.CompilerParams(
            collective_id=0, has_side_effects=True, vmem_limit_bytes=58 * 2**20
        ),
        name="layer",
    )(
        parents,
        node_lengths,
        token_leaf.reshape(1, tokens),
        activations,
        queries,
        norm_gain.reshape(1, width),
        tree_cache_keys,
        tree_cache_values,
        out_weight,
        gate_weight,
        up_weight,
        down_weight,
    )


def solution(mesh):
    return jax.shard_map(
        functools.partial(local, mesh.shape["kv"], mesh.shape["tp"]),
        mesh=mesh,
        in_specs=(
            P(("kv", "tp"), None),
            P("kv", "tp"),
            P("kv", "tp"),
            P("kv", "tp"),
            P(),
            P(),
            P(),
            P("tp", None),
            P(),
            P(None, ("kv", "tp")),
            P(None, ("kv", "tp")),
            P(("kv", "tp"), None),
        ),
        out_specs=P(("kv", "tp"), None),
        check_vma=False,
    )
```

```python
import functools
import math

import jax
import jax.numpy as jnp
from jax import lax
from jax.experimental import pallas as pl
from jax.experimental.pallas import tpu as pltpu
from jax.sharding import PartitionSpec as P

QUERY_HEADS = 40
KEY_VALUE_HEADS = 8
HEAD_WIDTH = 128
LOWEST = -1e30
EPSILON = 1e-06
MESH = pl.DeviceIdType.MESH
F32 = jnp.float32
BF16 = jnp.bfloat16


def copy_to(source, target, send, receive, axis, peer):
    return pltpu.make_async_remote_copy(
        src_ref=source,
        dst_ref=target,
        send_sem=send,
        recv_sem=receive,
        device_id={axis: peer},
        device_id_type=MESH,
    )


def layer_kernel(
    nk,
    nt,
    parts,
    parents,
    lengths,
    leaf_row,
    act,
    query,
    gain,
    keys_hbm,
    values_hbm,
    out_hbm,
    gate_hbm,
    up_hbm,
    down_hbm,
    result,
    keys,
    values,
    out_w,
    gate_w,
    up_w,
    down_w,
    q_all,
    act_all,
    w_send,
    w_recv,
    ml_send,
    ml_recv,
    p_send,
    p_recv,
    res,
    acc_gate,
    acc_up,
    s_send,
    s_recv,
    g_send,
    g_recv,
    f_send,
    f_recv,
    own,
    load_sem,
    q_ss,
    q_rs,
    a_ss,
    a_rs,
    w_ss,
    w_rs,
    ml_ss,
    ml_rs,
    p_ss,
    p_rs,
    rt_ss,
    rt_rs,
    rk_ss,
    rk_rs,
    s_ss,
    s_rs,
    g_ss,
    g_rs,
    f_ss,
    f_rs,
):
    k_me = lax.axis_index("kv")
    t_me = lax.axis_index("tp")
    group, q_width = query.shape
    tokens = nk * group
    slots = keys.shape[0]
    kv_local = keys.shape[1] // HEAD_WIDTH
    per_kv = QUERY_HEADS // KEY_VALUE_HEADS
    width = act.shape[1]
    rows_own = act.shape[0]
    cols = width // nt

    loads = [
        pltpu.make_async_copy(source, target, load_sem.at[i])
        for i, (source, target) in enumerate(
            (
                (keys_hbm, keys),
                (values_hbm, values),
                (out_hbm, out_w),
                (gate_hbm, gate_w),
                (up_hbm, up_w),
                (down_hbm, down_w),
            )
        )
    ]
    for load in loads:
        load.start()

    q_all[k_me] = query[...]
    act_all[t_me] = act[...].astype(F32)

    barrier = pltpu.get_barrier_semaphore()
    for d in range(1, nk):
        pl.semaphore_signal(
            barrier, inc=1, device_id={"kv": lax.rem(k_me + d, nk)}, device_id_type=MESH
        )
    for d in range(1, nt):
        pl.semaphore_signal(
            barrier, inc=1, device_id={"tp": lax.rem(t_me + d, nt)}, device_id_type=MESH
        )
    pl.semaphore_wait(barrier, nk + nt - 2)

    kv_to = [lax.rem(k_me + d, nk) for d in range(nk)]
    kv_from = [lax.rem(k_me + nk - d, nk) for d in range(nk)]
    tp_to = [lax.rem(t_me + d, nt) for d in range(nt)]
    tp_from = [lax.rem(t_me + nt - d, nt) for d in range(nt)]
    sends = []

    def send(*args):
        copy = copy_to(*args)
        copy.start()
        sends.append(copy)

    for d in range(1, nk):
        send(q_all.at[k_me], q_all.at[k_me], q_ss.at[d], q_rs.at[d], "kv", kv_to[d])
    for d in range(1, nt):
        send(act_all.at[t_me], act_all.at[t_me], a_ss.at[d], a_rs.at[d], "tp", tp_to[d])

    slot_id = k_me * slots + lax.broadcasted_iota(jnp.int32, (1, slots), 1)
    node = jnp.zeros((1, slots), jnp.int32)
    end = jnp.int32(0)
    nodes = parents.shape[0]
    for n in range(nodes):
        end = end + lengths[n]
        node = node + jnp.where(slot_id >= end, 1, 0)
    node = jnp.where(node == nodes, -1, node)
    diagonal = lax.broadcasted_iota(jnp.int32, (tokens, tokens), 0) == lax.broadcasted_iota(
        jnp.int32, (tokens, tokens), 1
    )
    leaf = jnp.sum(
        jnp.where(diagonal, jnp.broadcast_to(leaf_row[...], (tokens, tokens)), 0),
        axis=1,
        keepdims=True,
    )
    tenant = jnp.zeros_like(leaf)
    for n in range(nodes):
        tenant = tenant + jnp.where(leaf == n, parents[n], 0)
    allowed = ((node == 0) | (node == tenant) | (node == leaf))[None]

    loads[0].wait()
    loads[1].wait()
    for d in range(1, nk):
        block = q_all.at[kv_from[d]]
        copy_to(block, block, q_ss.at[d], q_rs.at[d], "kv", kv_to[d]).wait_recv()

    lane = lax.broadcasted_iota(jnp.int32, (tokens, HEAD_WIDTH), 1)
    tops = jnp.zeros((tokens, HEAD_WIDTH), F32)
    sums = jnp.ones((tokens, HEAD_WIDTH), F32)
    for j in range(kv_local):
        stacked = jnp.concatenate(
            [
                q_all[:, :, h * HEAD_WIDTH : (h + 1) * HEAD_WIDTH]
                .astype(F32)
                .reshape(tokens, HEAD_WIDTH)
                for h in range(j * per_kv, (j + 1) * per_kv)
            ],
            axis=0,
        ).astype(BF16)
        head = slice(j * HEAD_WIDTH, (j + 1) * HEAD_WIDTH)
        scores = lax.dot_general(
            stacked, keys[:, head], (((1,), (1,)), ((), ())), preferred_element_type=F32
        ) * (1.0 / math.sqrt(HEAD_WIDTH))
        scores = scores.reshape(per_kv, tokens, slots)
        top = jnp.max(jnp.where(allowed, scores, LOWEST), axis=2, keepdims=True)
        weights = jnp.where(allowed, jnp.exp(jnp.minimum(scores - top, 0.0)), 0.0)
        total = jnp.sum(weights, axis=2, keepdims=True)
        weighted = jnp.dot(
            weights.astype(BF16).reshape(per_kv * tokens, slots),
            values[:, head],
            preferred_element_type=F32,
        ).reshape(per_kv, nk, group, HEAD_WIDTH)
        for g in range(per_kv):
            h = j * per_kv + g
            w_send[:, :, h * HEAD_WIDTH : (h + 1) * HEAD_WIDTH] = weighted[g].astype(BF16)
            tops = jnp.where(lane == h, top[g], tops)
            sums = jnp.where(lane == h, total[g], sums)
    ml_send[:, 0] = tops.reshape(nk, group, HEAD_WIDTH)
    ml_send[:, 1] = sums.reshape(nk, group, HEAD_WIDTH)

    for d in range(1, nk):
        send(ml_send.at[kv_to[d]], ml_recv.at[d], ml_ss.at[d], ml_rs.at[d], "kv", kv_to[d])
        send(w_send.at[kv_to[d]], w_recv.at[d], w_ss.at[d], w_rs.at[d], "kv", kv_to[d])
    ml_recv[0] = ml_send[k_me]
    w_recv[0] = w_send[k_me]
    loads[2].wait()
    for d in range(1, nk):
        copy_to(
            ml_send.at[kv_to[d]], ml_recv.at[d], ml_ss.at[d], ml_rs.at[d], "kv", kv_to[d]
        ).wait_recv()
        copy_to(
            w_send.at[kv_to[d]], w_recv.at[d], w_ss.at[d], w_rs.at[d], "kv", kv_to[d]
        ).wait_recv()
    highest = ml_recv[0, 0]
    for d in range(1, nk):
        highest = jnp.maximum(highest, ml_recv[d, 0])
    scales = [jnp.exp(ml_recv[d, 0] - highest) for d in range(nk)]
    denominator = scales[0] * ml_recv[0, 1]
    for d in range(1, nk):
        denominator = denominator + scales[d] * ml_recv[d, 1]
    pieces = []
    for h in range(kv_local * per_kv):
        total = jnp.zeros((group, HEAD_WIDTH), F32)
        for d in range(nk):
            part = w_recv[d, :, h * HEAD_WIDTH : (h + 1) * HEAD_WIDTH].astype(F32)
            total = total + part * scales[d][:, h : h + 1]
        pieces.append(total / denominator[:, h : h + 1])
    context = jnp.concatenate(pieces, axis=1).astype(BF16)

    for d in list(range(1, nt)) + [0]:
        at = pl.multiple_of(tp_to[d] * cols, 128)
        product = jnp.dot(context, out_w[:, pl.ds(at, cols)], preferred_element_type=F32)
        if d > 0:
            p_send[d] = product.astype(BF16)
            send(p_send.at[d], p_recv.at[d], p_ss.at[d], p_rs.at[d], "tp", tp_to[d])
    for d in range(1, nt):
        block = act_all.at[tp_from[d]]
        copy_to(block, block, a_ss.at[d], a_rs.at[d], "tp", tp_to[d]).wait_recv()
    mine = pl.ds(pl.multiple_of(t_me * cols, 128), cols)
    row = lax.broadcasted_iota(jnp.int32, (group, cols), 0)
    before = jnp.zeros((group, cols), F32)
    for t in range(nt):
        block = act_all[t, :, mine]
        for i in range(rows_own):
            before = jnp.where(
                row == t * rows_own + i, jnp.broadcast_to(block[i : i + 1], (group, cols)), before
            )
    attended = product
    for d in range(1, nt):
        copy_to(
            p_send.at[d], p_recv.at[d], p_ss.at[d], p_rs.at[d], "tp", tp_to[d]
        ).wait_recv()
        attended = attended + p_recv[d].astype(F32)
    res[k_me, t_me] = (before + attended).astype(BF16)

    block = res.at[k_me, t_me]
    for d in range(1, nt):
        send(block, block, rt_ss.at[d], rt_rs.at[d], "tp", tp_to[d])
    for e in range(nt):
        block = res.at[k_me, tp_from[e]]
        if e > 0:
            copy_to(block, block, rt_ss.at[e], rt_rs.at[e], "tp", tp_to[e]).wait_recv()
        for d in range(1, nk):
            send(block, block, rk_ss.at[e, d], rk_rs.at[e, d], "kv", kv_to[d])

    square = jnp.zeros((tokens, 1), F32)
    for e in range(nt):
        c = tp_from[e]
        for d in range(1, nk):
            block = res.at[kv_from[d], c]
            copy_to(block, block, rk_ss.at[e, d], rk_rs.at[e, d], "kv", kv_to[d]).wait_recv()
        at = pl.ds(pl.multiple_of(c * cols, 128), cols)
        part = res[:, c].astype(F32).reshape(tokens, cols)
        square = square + jnp.sum(part * part, axis=1, keepdims=True)
        x = (part * gain[:, at]).astype(BF16)
        for load, weight, acc in ((loads[3], gate_w, acc_gate), (loads[4], up_w, acc_up)):
            if e == 0:
                load.wait()
            product = lax.dot_general(
                x, weight[:, at], (((1,), (1,)), ((), ())), preferred_element_type=F32
            )
            acc[...] = product if e == 0 else acc[...] + product
    inverse = lax.rsqrt(square / width + EPSILON)
    gate = acc_gate[...] * inverse
    hidden = (gate / (1.0 + jnp.exp(-gate)) * (acc_up[...] * inverse)).astype(BF16)
    loads[5].wait()

    half = nk // 2
    odd = lax.rem(k_me, 2)
    m_me = k_me // 2
    partner = k_me + 1 - 2 * odd
    m_to = [lax.rem(m_me + d, half) for d in range(half)]
    chunk = width // parts

    def to_partner(c):
        return copy_to(
            s_send.at[c, 1 - odd], s_recv.at[c], s_ss.at[c], s_rs.at[c], "kv", partner
        )

    def to_others(c, d):
        return copy_to(
            g_send.at[c, m_to[d]],
            g_recv.at[c, d],
            g_ss.at[c, d],
            g_rs.at[c, d],
            "kv",
            2 * m_to[d] + odd,
        )

    for c in range(parts + 1):
        if c < parts:
            product = jnp.dot(
                hidden, down_w[:, c * chunk : (c + 1) * chunk], preferred_element_type=F32
            ).reshape(half, 2, group, chunk)
            s_send[c, 0] = product[:, 0].astype(BF16)
            s_send[c, 1] = product[:, 1].astype(BF16)
            copy = to_partner(c)
            copy.start()
            sends.append(copy)
        if c > 0:
            to_partner(c - 1).wait_recv()
            g_send[c - 1] = (s_send[c - 1, odd].astype(F32) + s_recv[c - 1].astype(F32)).astype(
                BF16
            )
            for d in range(1, half):
                copy = to_others(c - 1, d)
                copy.start()
                sends.append(copy)

    row = lax.broadcasted_iota(jnp.int32, (group, cols), 0)
    for c in range(parts):
        mixed = g_send[c, m_me].astype(F32)
        for d in range(1, half):
            to_others(c, d).wait_recv()
            mixed = mixed + g_recv[c, d].astype(F32)
        for t in range(nt):
            f_send[c, t] = mixed[t * rows_own : (t + 1) * rows_own].astype(BF16)
        for d in range(1, nt):
            send(
                f_send.at[c, tp_to[d]],
                f_recv.at[c, d],
                f_ss.at[c, d],
                f_rs.at[c, d],
                "tp",
                tp_to[d],
            )
        for b in range(chunk // cols):
            first = c * (chunk // cols) + b
            here = mixed[:, b * cols : (b + 1) * cols] + res[k_me, first].astype(F32)
            for i in range(rows_own):
                own[i : i + 1, first * cols : (first + 1) * cols] = jnp.sum(
                    jnp.where(row == t_me * rows_own + i, here, 0.0), axis=0, keepdims=True
                )
    for c in range(parts):
        at = slice(c * chunk, (c + 1) * chunk)
        total = own[:, at]
        for d in range(1, nt):
            copy_to(
                f_send.at[c, tp_to[d]],
                f_recv.at[c, d],
                f_ss.at[c, d],
                f_rs.at[c, d],
                "tp",
                tp_to[d],
            ).wait_recv()
            total = total + f_recv[c, d].astype(F32)
        result[:, at] = total
    for copy in sends:
        copy.wait_send()


def local(
    nk,
    nt,
    activations,
    queries,
    tree_cache_keys,
    tree_cache_values,
    parents,
    node_lengths,
    token_leaf,
    out_weight,
    norm_gain,
    gate_weight,
    up_weight,
    down_weight,
):
    group, q_width = queries.shape
    rows_own, width = activations.shape
    tokens = nk * group
    cols = width // nt
    units = gate_weight.shape[1]
    parts = 4
    chunk = width // parts
    dma = pltpu.SemaphoreType.DMA
    vmem = pl.BlockSpec(memory_space=pltpu.VMEM)
    smem = pl.BlockSpec(memory_space=pltpu.SMEM)
    anywhere = pl.BlockSpec(memory_space=pl.ANY)
    return pl.pallas_call(
        functools.partial(layer_kernel, nk, nt, parts),
        out_shape=jax.ShapeDtypeStruct((rows_own, width), F32),
        in_specs=[smem, smem, vmem, vmem, vmem, vmem] + [anywhere] * 6,
        out_specs=vmem,
        scratch_shapes=[
            pltpu.VMEM(tree_cache_keys.shape, BF16),
            pltpu.VMEM(tree_cache_values.shape, BF16),
            pltpu.VMEM(out_weight.shape, BF16),
            pltpu.VMEM((units, width), BF16),
            pltpu.VMEM((units, width), BF16),
            pltpu.VMEM(down_weight.shape, BF16),
            pltpu.VMEM((nk, group, q_width), BF16),
            pltpu.VMEM((nt, rows_own, width), F32),
            pltpu.VMEM((nk, group, q_width), BF16),
            pltpu.VMEM((nk, group, q_width), BF16),
            pltpu.VMEM((nk, 2, group, HEAD_WIDTH), F32),
            pltpu.VMEM((nk, 2, group, HEAD_WIDTH), F32),
            pltpu.VMEM((nt, group, cols), BF16),
            pltpu.VMEM((nt, group, cols), BF16),
            pltpu.VMEM((nk, nt, group, cols), BF16),
            pltpu.VMEM((tokens, units), F32),
            pltpu.VMEM((tokens, units), F32),
            pltpu.VMEM((parts, 2, nk // 2, group, chunk), BF16),
            pltpu.VMEM((parts, nk // 2, group, chunk), BF16),
            pltpu.VMEM((parts, nk // 2, group, chunk), BF16),
            pltpu.VMEM((parts, nk // 2, group, chunk), BF16),
            pltpu.VMEM((parts, nt, rows_own, chunk), BF16),
            pltpu.VMEM((parts, nt, rows_own, chunk), BF16),
            pltpu.VMEM((rows_own, width), F32),
            dma((6,)),
            dma((nk,)),
            dma((nk,)),
            dma((nt,)),
            dma((nt,)),
            dma((nk,)),
            dma((nk,)),
            dma((nk,)),
            dma((nk,)),
            dma((nt,)),
            dma((nt,)),
            dma((nt,)),
            dma((nt,)),
            dma((nt, nk)),
            dma((nt, nk)),
            dma((parts,)),
            dma((parts,)),
            dma((parts, nk // 2)),
            dma((parts, nk // 2)),
            dma((parts, nt)),
            dma((parts, nt)),
        ],
        compiler_params=pltpu.CompilerParams(
            collective_id=0, has_side_effects=True, vmem_limit_bytes=58 * 2**20
        ),
        name="layer",
    )(
        parents,
        node_lengths,
        token_leaf.reshape(1, tokens),
        activations,
        queries,
        norm_gain.reshape(1, width),
        tree_cache_keys,
        tree_cache_values,
        out_weight,
        gate_weight.T,
        up_weight.T,
        down_weight,
    ).astype(BF16)


def solution(mesh):
    return jax.shard_map(
        functools.partial(local, mesh.shape["kv"], mesh.shape["tp"]),
        mesh=mesh,
        in_specs=(
            P(("kv", "tp"), None),
            P("kv", "tp"),
            P("kv", "tp"),
            P("kv", "tp"),
            P(),
            P(),
            P(),
            P("tp", None),
            P(),
            P(None, ("kv", "tp")),
            P(None, ("kv", "tp")),
            P(("kv", "tp"), None),
        ),
        out_specs=P(("kv", "tp"), None),
        check_vma=False,
    )
```

```python
import functools
import math

import jax
import jax.numpy as jnp
from jax import lax
from jax.experimental import pallas as pl
from jax.experimental.pallas import tpu as pltpu
from jax.sharding import PartitionSpec as P

QUERY_HEADS = 40
KEY_VALUE_HEADS = 8
HEAD_WIDTH = 128
LOWEST = -1e30
EPSILON = 1e-06
MESH = pl.DeviceIdType.MESH
F32 = jnp.float32
BF16 = jnp.bfloat16


def copy_to(source, target, send, receive, axis, peer):
    return pltpu.make_async_remote_copy(
        src_ref=source,
        dst_ref=target,
        send_sem=send,
        recv_sem=receive,
        device_id={axis: peer},
        device_id_type=MESH,
    )


def layer_kernel(
    nk,
    nt,
    parts,
    parents,
    lengths,
    leaf_row,
    act,
    query,
    gain,
    keys_hbm,
    values_hbm,
    out_hbm,
    gate_hbm,
    up_hbm,
    down_hbm,
    result,
    keys,
    values,
    out_w,
    gate_w,
    up_w,
    down_w,
    q_all,
    act_all,
    w_send,
    w_recv,
    ml_send,
    ml_recv,
    p_send,
    p_recv,
    res,
    acc_gate,
    acc_up,
    s_send,
    s_recv,
    g_send,
    g_recv,
    f_send,
    f_recv,
    own,
    load_sem,
    q_ss,
    q_rs,
    a_ss,
    a_rs,
    w_ss,
    w_rs,
    ml_ss,
    ml_rs,
    p_ss,
    p_rs,
    rt_ss,
    rt_rs,
    rk_ss,
    rk_rs,
    rp_ss,
    rp_rs,
    s_ss,
    s_rs,
    g_ss,
    g_rs,
    f_ss,
    f_rs,
):
    k_me = lax.axis_index("kv")
    t_me = lax.axis_index("tp")
    group, q_width = query.shape
    tokens = nk * group
    slots = keys.shape[0]
    kv_local = keys.shape[1] // HEAD_WIDTH
    per_kv = QUERY_HEADS // KEY_VALUE_HEADS
    width = act.shape[1]
    rows_own = act.shape[0]
    cols = width // nt

    loads = [
        pltpu.make_async_copy(source, target, load_sem.at[i])
        for i, (source, target) in enumerate(
            (
                (keys_hbm, keys),
                (values_hbm, values),
                (out_hbm, out_w),
                (gate_hbm, gate_w),
                (up_hbm, up_w),
                (down_hbm, down_w),
            )
        )
    ]
    for load in loads:
        load.start()

    q_all[k_me] = query[...]
    act_all[t_me] = act[...].astype(F32)

    barrier = pltpu.get_barrier_semaphore()
    for d in range(1, nk):
        pl.semaphore_signal(
            barrier, inc=1, device_id={"kv": lax.rem(k_me + d, nk)}, device_id_type=MESH
        )
    for d in range(1, nt):
        pl.semaphore_signal(
            barrier, inc=1, device_id={"tp": lax.rem(t_me + d, nt)}, device_id_type=MESH
        )
    pl.semaphore_wait(barrier, nk + nt - 2)

    kv_to = [lax.rem(k_me + d, nk) for d in range(nk)]
    kv_from = [lax.rem(k_me + nk - d, nk) for d in range(nk)]
    tp_to = [lax.rem(t_me + d, nt) for d in range(nt)]
    tp_from = [lax.rem(t_me + nt - d, nt) for d in range(nt)]
    half = nk // 2
    odd = lax.rem(k_me, 2)
    m_me = k_me // 2
    partner = k_me + 1 - 2 * odd
    m_to = [lax.rem(m_me + d, half) for d in range(half)]
    m_from = [lax.rem(m_me + half - d, half) for d in range(half)]
    sends = []

    def send(*args):
        copy = copy_to(*args)
        copy.start()
        sends.append(copy)

    for d in range(1, nk):
        send(q_all.at[k_me], q_all.at[k_me], q_ss.at[d], q_rs.at[d], "kv", kv_to[d])
    for d in range(1, nt):
        send(act_all.at[t_me], act_all.at[t_me], a_ss.at[d], a_rs.at[d], "tp", tp_to[d])

    slot_id = k_me * slots + lax.broadcasted_iota(jnp.int32, (1, slots), 1)
    node = jnp.zeros((1, slots), jnp.int32)
    end = jnp.int32(0)
    nodes = parents.shape[0]
    for n in range(nodes):
        end = end + lengths[n]
        node = node + jnp.where(slot_id >= end, 1, 0)
    node = jnp.where(node == nodes, -1, node)
    diagonal = lax.broadcasted_iota(jnp.int32, (tokens, tokens), 0) == lax.broadcasted_iota(
        jnp.int32, (tokens, tokens), 1
    )
    leaf = jnp.sum(
        jnp.where(diagonal, jnp.broadcast_to(leaf_row[...], (tokens, tokens)), 0),
        axis=1,
        keepdims=True,
    )
    tenant = jnp.zeros_like(leaf)
    for n in range(nodes):
        tenant = tenant + jnp.where(leaf == n, parents[n], 0)
    bias = jnp.where((node == 0) | (node == tenant) | (node == leaf), 0.0, LOWEST)[None]

    loads[0].wait()
    loads[1].wait()
    for d in range(1, nk):
        block = q_all.at[kv_from[d]]
        copy_to(block, block, q_ss.at[d], q_rs.at[d], "kv", kv_to[d]).wait_recv()

    lane = lax.broadcasted_iota(jnp.int32, (tokens, HEAD_WIDTH), 1)
    tops = jnp.zeros((tokens, HEAD_WIDTH), F32)
    sums = jnp.ones((tokens, HEAD_WIDTH), F32)
    for j in range(kv_local):
        stacked = jnp.concatenate(
            [
                q_all[:, :, h * HEAD_WIDTH : (h + 1) * HEAD_WIDTH]
                .astype(F32)
                .reshape(tokens, HEAD_WIDTH)
                for h in range(j * per_kv, (j + 1) * per_kv)
            ],
            axis=0,
        ).astype(BF16)
        head = slice(j * HEAD_WIDTH, (j + 1) * HEAD_WIDTH)
        scores = lax.dot_general(
            stacked, keys[:, head], (((1,), (1,)), ((), ())), preferred_element_type=F32
        ) * (1.0 / math.sqrt(HEAD_WIDTH))
        scores = scores.reshape(per_kv, tokens, slots) + bias
        top = jnp.max(scores, axis=2, keepdims=True)
        weights = jnp.exp(scores - top)
        total = jnp.sum(weights, axis=2, keepdims=True)
        weighted = jnp.dot(
            weights.astype(BF16).reshape(per_kv * tokens, slots),
            values[:, head],
            preferred_element_type=F32,
        ).reshape(per_kv, nk, group, HEAD_WIDTH)
        for g in range(per_kv):
            h = j * per_kv + g
            w_send[j, :, :, g * HEAD_WIDTH : (g + 1) * HEAD_WIDTH] = weighted[g].astype(BF16)
            tops = jnp.where(lane == h, top[g], tops)
            sums = jnp.where(lane == h, total[g], sums)
        if j == kv_local - 1:
            ml_send[:, 0] = tops.reshape(nk, group, HEAD_WIDTH)
            ml_send[:, 1] = sums.reshape(nk, group, HEAD_WIDTH)
            for d in range(1, nk):
                send(ml_send.at[kv_to[d]], ml_recv.at[d], ml_ss.at[d], ml_rs.at[d], "kv", kv_to[d])
        for d in range(1, nk):
            send(
                w_send.at[j, kv_to[d]],
                w_recv.at[j, d],
                w_ss.at[j, d],
                w_rs.at[j, d],
                "kv",
                kv_to[d],
            )
    ml_recv[0] = ml_send[k_me]
    for j in range(kv_local):
        w_recv[j, 0] = w_send[j, k_me]
    loads[2].wait()
    for d in range(1, nk):
        copy_to(
            ml_send.at[kv_to[d]], ml_recv.at[d], ml_ss.at[d], ml_rs.at[d], "kv", kv_to[d]
        ).wait_recv()
        for j in range(kv_local):
            copy_to(
                w_send.at[j, kv_to[d]],
                w_recv.at[j, d],
                w_ss.at[j, d],
                w_rs.at[j, d],
                "kv",
                kv_to[d],
            ).wait_recv()
    highest = ml_recv[0, 0]
    for d in range(1, nk):
        highest = jnp.maximum(highest, ml_recv[d, 0])
    scales = [jnp.exp(ml_recv[d, 0] - highest) for d in range(nk)]
    denominator = scales[0] * ml_recv[0, 1]
    for d in range(1, nk):
        denominator = denominator + scales[d] * ml_recv[d, 1]
    pieces = []
    for h in range(kv_local * per_kv):
        total = jnp.zeros((group, HEAD_WIDTH), F32)
        j, g = divmod(h, per_kv)
        for d in range(nk):
            part = w_recv[j, d, :, g * HEAD_WIDTH : (g + 1) * HEAD_WIDTH].astype(F32)
            total = total + part * scales[d][:, h : h + 1]
        pieces.append(total / denominator[:, h : h + 1])
    context = jnp.concatenate(pieces, axis=1).astype(BF16)

    for d in list(range(1, nt)) + [0]:
        at = pl.multiple_of(tp_to[d] * cols, 128)
        product = jnp.dot(context, out_w[:, pl.ds(at, cols)], preferred_element_type=F32)
        if d > 0:
            p_send[d] = product.astype(BF16)
            send(p_send.at[d], p_recv.at[d], p_ss.at[d], p_rs.at[d], "tp", tp_to[d])
    for d in range(1, nt):
        block = act_all.at[tp_from[d]]
        copy_to(block, block, a_ss.at[d], a_rs.at[d], "tp", tp_to[d]).wait_recv()
    mine = pl.ds(pl.multiple_of(t_me * cols, 128), cols)
    row = lax.broadcasted_iota(jnp.int32, (group, cols), 0)
    before = jnp.zeros((group, cols), F32)
    for t in range(nt):
        block = act_all[t, :, mine]
        for i in range(rows_own):
            before = jnp.where(
                row == t * rows_own + i, jnp.broadcast_to(block[i : i + 1], (group, cols)), before
            )
    attended = product
    for d in range(1, nt):
        copy_to(
            p_send.at[d], p_recv.at[d], p_ss.at[d], p_rs.at[d], "tp", tp_to[d]
        ).wait_recv()
        attended = attended + p_recv[d].astype(F32)
    res[k_me, t_me] = (before + attended).astype(BF16)

    block = res.at[k_me, t_me]
    for d in range(1, nt):
        send(block, block, rt_ss.at[d], rt_rs.at[d], "tp", tp_to[d])
    for e in range(nt):
        block = res.at[k_me, tp_from[e]]
        if e > 0:
            copy_to(block, block, rt_ss.at[e], rt_rs.at[e], "tp", tp_to[e]).wait_recv()
        send(block, block, rp_ss.at[e, 0], rp_rs.at[e, 0], "kv", partner)
        for d in range(1, half):
            send(block, block, rk_ss.at[e, d], rk_rs.at[e, d], "kv", 2 * m_to[d] + odd)

    def forward(e):
        for d in range(1, half):
            block = res.at[2 * m_from[d] + odd, tp_from[e]]
            copy_to(
                block, block, rk_ss.at[e, d], rk_rs.at[e, d], "kv", 2 * m_to[d] + odd
            ).wait_recv()
            send(block, block, rp_ss.at[e, d], rp_rs.at[e, d], "kv", partner)

    square = jnp.zeros((tokens, 1), F32)
    forward(0)
    for e in range(nt):
        c = tp_from[e]
        for d in range(half):
            block = res.at[2 * m_from[d] + 1 - odd, c]
            copy_to(block, block, rp_ss.at[e, d], rp_rs.at[e, d], "kv", partner).wait_recv()
        at = pl.ds(pl.multiple_of(c * cols, 128), cols)
        part = res[:, c].astype(F32).reshape(tokens, cols)
        square = square + jnp.sum(part * part, axis=1, keepdims=True)
        x = (part * gain[:, at]).astype(BF16)
        for load, weight, acc in ((loads[3], gate_w, acc_gate), (loads[4], up_w, acc_up)):
            if e == 0:
                load.wait()
            product = lax.dot_general(
                x, weight[:, at], (((1,), (1,)), ((), ())), preferred_element_type=F32
            )
            acc[...] = product if e == 0 else acc[...] + product
            if acc is acc_gate and e + 1 < nt:
                forward(e + 1)
    inverse = lax.rsqrt(square / width + EPSILON)
    gate = acc_gate[...] * inverse
    hidden = (gate / (1.0 + jnp.exp(-gate)) * (acc_up[...] * inverse)).astype(BF16)
    loads[5].wait()

    chunk = width // parts

    def to_partner(c):
        return copy_to(
            s_send.at[c, 1 - odd], s_recv.at[c], s_ss.at[c], s_rs.at[c], "kv", partner
        )

    def to_others(c, d):
        return copy_to(
            g_send.at[c, m_to[d]],
            g_recv.at[c, d],
            g_ss.at[c, d],
            g_rs.at[c, d],
            "kv",
            2 * m_to[d] + odd,
        )

    for c in range(parts + 1):
        if c < parts:
            product = jnp.dot(
                hidden, down_w[:, c * chunk : (c + 1) * chunk], preferred_element_type=F32
            ).reshape(half, 2, group, chunk)
            s_send[c, 0] = product[:, 0].astype(BF16)
            s_send[c, 1] = product[:, 1].astype(BF16)
            copy = to_partner(c)
            copy.start()
            sends.append(copy)
        if c > 0:
            to_partner(c - 1).wait_recv()
            g_send[c - 1] = (s_send[c - 1, odd].astype(F32) + s_recv[c - 1].astype(F32)).astype(
                BF16
            )
            for d in range(1, half):
                copy = to_others(c - 1, d)
                copy.start()
                sends.append(copy)

    row = lax.broadcasted_iota(jnp.int32, (group, cols), 0)
    for c in range(parts):
        mixed = g_send[c, m_me].astype(F32)
        for d in range(1, half):
            to_others(c, d).wait_recv()
            mixed = mixed + g_recv[c, d].astype(F32)
        for t in range(nt):
            f_send[c, t] = mixed[t * rows_own : (t + 1) * rows_own].astype(BF16)
        for d in range(1, nt):
            send(
                f_send.at[c, tp_to[d]],
                f_recv.at[c, d],
                f_ss.at[c, d],
                f_rs.at[c, d],
                "tp",
                tp_to[d],
            )
        for b in range(chunk // cols):
            first = c * (chunk // cols) + b
            here = mixed[:, b * cols : (b + 1) * cols] + res[k_me, first].astype(F32)
            for i in range(rows_own):
                own[i : i + 1, first * cols : (first + 1) * cols] = jnp.sum(
                    jnp.where(row == t_me * rows_own + i, here, 0.0), axis=0, keepdims=True
                )
    for c in range(parts):
        at = slice(c * chunk, (c + 1) * chunk)
        total = own[:, at]
        for d in range(1, nt):
            copy_to(
                f_send.at[c, tp_to[d]],
                f_recv.at[c, d],
                f_ss.at[c, d],
                f_rs.at[c, d],
                "tp",
                tp_to[d],
            ).wait_recv()
            total = total + f_recv[c, d].astype(F32)
        result[:, at] = total
    for copy in sends:
        copy.wait_send()


def local(
    nk,
    nt,
    activations,
    queries,
    tree_cache_keys,
    tree_cache_values,
    parents,
    node_lengths,
    token_leaf,
    out_weight,
    norm_gain,
    gate_weight,
    up_weight,
    down_weight,
):
    group, q_width = queries.shape
    rows_own, width = activations.shape
    tokens = nk * group
    cols = width // nt
    units = gate_weight.shape[1]
    kv_local = tree_cache_keys.shape[1] // HEAD_WIDTH
    parts = 4
    chunk = width // parts
    dma = pltpu.SemaphoreType.DMA
    vmem = pl.BlockSpec(memory_space=pltpu.VMEM)
    smem = pl.BlockSpec(memory_space=pltpu.SMEM)
    anywhere = pl.BlockSpec(memory_space=pl.ANY)
    return pl.pallas_call(
        functools.partial(layer_kernel, nk, nt, parts),
        out_shape=jax.ShapeDtypeStruct((rows_own, width), F32),
        in_specs=[smem, smem, vmem, vmem, vmem, vmem] + [anywhere] * 6,
        out_specs=vmem,
        scratch_shapes=[
            pltpu.VMEM(tree_cache_keys.shape, BF16),
            pltpu.VMEM(tree_cache_values.shape, BF16),
            pltpu.VMEM(out_weight.shape, BF16),
            pltpu.VMEM((units, width), BF16),
            pltpu.VMEM((units, width), BF16),
            pltpu.VMEM(down_weight.shape, BF16),
            pltpu.VMEM((nk, group, q_width), BF16),
            pltpu.VMEM((nt, rows_own, width), F32),
            pltpu.VMEM((kv_local, nk, group, q_width // kv_local), BF16),
            pltpu.VMEM((kv_local, nk, group, q_width // kv_local), BF16),
            pltpu.VMEM((nk, 2, group, HEAD_WIDTH), F32),
            pltpu.VMEM((nk, 2, group, HEAD_WIDTH), F32),
            pltpu.VMEM((nt, group, cols), BF16),
            pltpu.VMEM((nt, group, cols), BF16),
            pltpu.VMEM((nk, nt, group, cols), BF16),
            pltpu.VMEM((tokens, units), F32),
            pltpu.VMEM((tokens, units), F32),
            pltpu.VMEM((parts, 2, nk // 2, group, chunk), BF16),
            pltpu.VMEM((parts, nk // 2, group, chunk), BF16),
            pltpu.VMEM((parts, nk // 2, group, chunk), BF16),
            pltpu.VMEM((parts, nk // 2, group, chunk), BF16),
            pltpu.VMEM((parts, nt, rows_own, chunk), BF16),
            pltpu.VMEM((parts, nt, rows_own, chunk), BF16),
            pltpu.VMEM((rows_own, width), F32),
            dma((6,)),
            dma((nk,)),
            dma((nk,)),
            dma((nt,)),
            dma((nt,)),
            dma((kv_local, nk)),
            dma((kv_local, nk)),
            dma((nk,)),
            dma((nk,)),
            dma((nt,)),
            dma((nt,)),
            dma((nt,)),
            dma((nt,)),
            dma((nt, nk // 2)),
            dma((nt, nk // 2)),
            dma((nt, nk // 2)),
            dma((nt, nk // 2)),
            dma((parts,)),
            dma((parts,)),
            dma((parts, nk // 2)),
            dma((parts, nk // 2)),
            dma((parts, nt)),
            dma((parts, nt)),
        ],
        compiler_params=pltpu.CompilerParams(
            collective_id=0, has_side_effects=True, vmem_limit_bytes=58 * 2**20
        ),
        name="layer",
    )(
        parents,
        node_lengths,
        token_leaf.reshape(1, tokens),
        activations,
        queries,
        norm_gain.reshape(1, width),
        tree_cache_keys,
        tree_cache_values,
        out_weight,
        gate_weight.T,
        up_weight.T,
        down_weight,
    ).astype(BF16)


def solution(mesh):
    return jax.shard_map(
        functools.partial(local, mesh.shape["kv"], mesh.shape["tp"]),
        mesh=mesh,
        in_specs=(
            P(("kv", "tp"), None),
            P("kv", "tp"),
            P("kv", "tp"),
            P("kv", "tp"),
            P(),
            P(),
            P(),
            P("tp", None),
            P(),
            P(None, ("kv", "tp")),
            P(None, ("kv", "tp")),
            P(("kv", "tp"), None),
        ),
        out_specs=P(("kv", "tp"), None),
        check_vma=False,
    )
```

```python
import functools
import math

import jax
import jax.numpy as jnp
from jax import lax
from jax.experimental import pallas as pl
from jax.experimental.pallas import tpu as pltpu
from jax.sharding import PartitionSpec as P

QUERY_HEADS = 40
KEY_VALUE_HEADS = 8
HEAD_WIDTH = 128
LOWEST = -1e30
EPSILON = 1e-06
MESH = pl.DeviceIdType.MESH
F32 = jnp.float32
BF16 = jnp.bfloat16
LOAD_PIECES = 2


def copy_to(source, target, send, receive, axis, peer):
    return pltpu.make_async_remote_copy(
        src_ref=source,
        dst_ref=target,
        send_sem=send,
        recv_sem=receive,
        device_id={axis: peer},
        device_id_type=MESH,
    )


def layer_kernel(
    nk,
    nt,
    parts,
    parents,
    lengths,
    leaf_row,
    act,
    query,
    gain,
    keys_hbm,
    values_hbm,
    out_hbm,
    gate_hbm,
    up_hbm,
    down_hbm,
    result,
    keys,
    values,
    out_w,
    gate_w,
    up_w,
    down_w,
    q_all,
    act_all,
    w_send,
    w_recv,
    ml_send,
    ml_recv,
    p_send,
    p_recv,
    res,
    acc_gate,
    acc_up,
    s_send,
    s_recv,
    g_send,
    g_recv,
    f_send,
    f_recv,
    own,
    load_sem,
    q_ss,
    q_rs,
    a_ss,
    a_rs,
    w_ss,
    w_rs,
    ml_ss,
    ml_rs,
    p_ss,
    p_rs,
    rt_ss,
    rt_rs,
    rk_ss,
    rk_rs,
    s_ss,
    s_rs,
    g_ss,
    g_rs,
    f_ss,
    f_rs,
):
    k_me = lax.axis_index("kv")
    t_me = lax.axis_index("tp")
    group, q_width = query.shape
    tokens = nk * group
    slots = keys.shape[0]
    kv_local = keys.shape[1] // HEAD_WIDTH
    per_kv = QUERY_HEADS // KEY_VALUE_HEADS
    width = act.shape[1]
    rows_own = act.shape[0]
    cols = width // nt

    loads = []
    for source, target in (
        (keys_hbm, keys),
        (values_hbm, values),
        (out_hbm, out_w),
        (gate_hbm, gate_w),
        (up_hbm, up_w),
        (down_hbm, down_w),
    ):
        rows = source.shape[0]
        pieces = LOAD_PIECES if rows % (LOAD_PIECES * 16) == 0 else 1
        size = rows // pieces
        loads.append(
            [
                pltpu.make_async_copy(
                    source.at[pl.ds(i * size, size)],
                    target.at[pl.ds(i * size, size)],
                    load_sem.at[len(loads), i],
                )
                for i in range(pieces)
            ]
        )

    def start(which):
        for copy in loads[which]:
            copy.start()

    def loaded(which):
        for copy in loads[which]:
            copy.wait()

    for which in range(3):
        start(which)

    q_all[k_me] = query[...]
    act_all[t_me] = act[...].astype(F32)

    barrier = pltpu.get_barrier_semaphore()
    for d in range(1, nk):
        pl.semaphore_signal(
            barrier, inc=1, device_id={"kv": lax.rem(k_me + d, nk)}, device_id_type=MESH
        )
    for d in range(1, nt):
        pl.semaphore_signal(
            barrier, inc=1, device_id={"tp": lax.rem(t_me + d, nt)}, device_id_type=MESH
        )
    pl.semaphore_wait(barrier, nk + nt - 2)

    kv_to = [lax.rem(k_me + d, nk) for d in range(nk)]
    kv_from = [lax.rem(k_me + nk - d, nk) for d in range(nk)]
    tp_to = [lax.rem(t_me + d, nt) for d in range(nt)]
    tp_from = [lax.rem(t_me + nt - d, nt) for d in range(nt)]
    sends = []

    def send(*args):
        copy = copy_to(*args)
        copy.start()
        sends.append(copy)

    for d in range(1, nk):
        send(q_all.at[k_me], q_all.at[k_me], q_ss.at[d], q_rs.at[d], "kv", kv_to[d])
    for d in range(1, nt):
        send(act_all.at[t_me], act_all.at[t_me], a_ss.at[d], a_rs.at[d], "tp", tp_to[d])

    slot_id = k_me * slots + lax.broadcasted_iota(jnp.int32, (1, slots), 1)
    node = jnp.zeros((1, slots), jnp.int32)
    end = jnp.int32(0)
    nodes = parents.shape[0]
    for n in range(nodes):
        end = end + lengths[n]
        node = node + jnp.where(slot_id >= end, 1, 0)
    node = jnp.where(node == nodes, -1, node)
    diagonal = lax.broadcasted_iota(jnp.int32, (tokens, tokens), 0) == lax.broadcasted_iota(
        jnp.int32, (tokens, tokens), 1
    )
    leaf = jnp.sum(
        jnp.where(diagonal, jnp.broadcast_to(leaf_row[...], (tokens, tokens)), 0),
        axis=1,
        keepdims=True,
    )
    tenant = jnp.zeros_like(leaf)
    for n in range(nodes):
        tenant = tenant + jnp.where(leaf == n, parents[n], 0)
    bias = jnp.where((node == 0) | (node == tenant) | (node == leaf), 0.0, LOWEST)[None]

    loaded(0)
    loaded(1)
    for d in range(1, nk):
        block = q_all.at[kv_from[d]]
        copy_to(block, block, q_ss.at[d], q_rs.at[d], "kv", kv_to[d]).wait_recv()

    for which in range(3, 6):
        start(which)

    lane = lax.broadcasted_iota(jnp.int32, (tokens, HEAD_WIDTH), 1)
    tops = jnp.zeros((tokens, HEAD_WIDTH), F32)
    sums = jnp.ones((tokens, HEAD_WIDTH), F32)
    for j in range(kv_local):
        stacked = jnp.concatenate(
            [
                q_all[:, :, h * HEAD_WIDTH : (h + 1) * HEAD_WIDTH]
                .astype(F32)
                .reshape(tokens, HEAD_WIDTH)
                for h in range(j * per_kv, (j + 1) * per_kv)
            ],
            axis=0,
        ).astype(BF16)
        head = slice(j * HEAD_WIDTH, (j + 1) * HEAD_WIDTH)
        scores = lax.dot_general(
            stacked, keys[:, head], (((1,), (1,)), ((), ())), preferred_element_type=F32
        ) * (1.0 / math.sqrt(HEAD_WIDTH))
        scores = scores.reshape(per_kv, tokens, slots) + bias
        top = jnp.max(scores, axis=2, keepdims=True)
        weights = jnp.exp(scores - top)
        total = jnp.sum(weights, axis=2, keepdims=True)
        weighted = jnp.dot(
            weights.astype(BF16).reshape(per_kv * tokens, slots),
            values[:, head],
            preferred_element_type=F32,
        ).reshape(per_kv, nk, group, HEAD_WIDTH)
        for g in range(per_kv):
            h = j * per_kv + g
            w_send[:, :, h * HEAD_WIDTH : (h + 1) * HEAD_WIDTH] = weighted[g].astype(BF16)
            tops = jnp.where(lane == h, top[g], tops)
            sums = jnp.where(lane == h, total[g], sums)
    ml_send[:, 0] = tops.reshape(nk, group, HEAD_WIDTH)
    ml_send[:, 1] = sums.reshape(nk, group, HEAD_WIDTH)

    for d in range(1, nk):
        send(ml_send.at[kv_to[d]], ml_recv.at[d], ml_ss.at[d], ml_rs.at[d], "kv", kv_to[d])
        send(w_send.at[kv_to[d]], w_recv.at[d], w_ss.at[d], w_rs.at[d], "kv", kv_to[d])
    ml_recv[0] = ml_send[k_me]
    w_recv[0] = w_send[k_me]
    loaded(2)
    for d in range(1, nk):
        copy_to(
            ml_send.at[kv_to[d]], ml_recv.at[d], ml_ss.at[d], ml_rs.at[d], "kv", kv_to[d]
        ).wait_recv()
        copy_to(
            w_send.at[kv_to[d]], w_recv.at[d], w_ss.at[d], w_rs.at[d], "kv", kv_to[d]
        ).wait_recv()
    highest = ml_recv[0, 0]
    for d in range(1, nk):
        highest = jnp.maximum(highest, ml_recv[d, 0])
    scales = [jnp.exp(ml_recv[d, 0] - highest) for d in range(nk)]
    denominator = scales[0] * ml_recv[0, 1]
    for d in range(1, nk):
        denominator = denominator + scales[d] * ml_recv[d, 1]
    pieces = []
    for h in range(kv_local * per_kv):
        total = jnp.zeros((group, HEAD_WIDTH), F32)
        for d in range(nk):
            part = w_recv[d, :, h * HEAD_WIDTH : (h + 1) * HEAD_WIDTH].astype(F32)
            total = total + part * scales[d][:, h : h + 1]
        pieces.append(total / denominator[:, h : h + 1])
    context = jnp.concatenate(pieces, axis=1).astype(BF16)

    for d in list(range(1, nt)) + [0]:
        at = pl.multiple_of(tp_to[d] * cols, 128)
        product = jnp.dot(context, out_w[:, pl.ds(at, cols)], preferred_element_type=F32)
        if d > 0:
            p_send[d] = product.astype(BF16)
            send(p_send.at[d], p_recv.at[d], p_ss.at[d], p_rs.at[d], "tp", tp_to[d])
    for d in range(1, nt):
        block = act_all.at[tp_from[d]]
        copy_to(block, block, a_ss.at[d], a_rs.at[d], "tp", tp_to[d]).wait_recv()
    mine = pl.ds(pl.multiple_of(t_me * cols, 128), cols)
    row = lax.broadcasted_iota(jnp.int32, (group, cols), 0)
    before = jnp.zeros((group, cols), F32)
    for t in range(nt):
        block = act_all[t, :, mine]
        for i in range(rows_own):
            before = jnp.where(
                row == t * rows_own + i, jnp.broadcast_to(block[i : i + 1], (group, cols)), before
            )
    attended = product
    for d in range(1, nt):
        copy_to(
            p_send.at[d], p_recv.at[d], p_ss.at[d], p_rs.at[d], "tp", tp_to[d]
        ).wait_recv()
        attended = attended + p_recv[d].astype(F32)
    res[k_me, t_me] = (before + attended).astype(BF16)

    block = res.at[k_me, t_me]
    for d in range(1, nt):
        send(block, block, rt_ss.at[d], rt_rs.at[d], "tp", tp_to[d])
    for e in range(nt):
        block = res.at[k_me, tp_from[e]]
        if e > 0:
            copy_to(block, block, rt_ss.at[e], rt_rs.at[e], "tp", tp_to[e]).wait_recv()
        for d in range(1, nk):
            send(block, block, rk_ss.at[e, d], rk_rs.at[e, d], "kv", kv_to[d])

    square = jnp.zeros((tokens, 1), F32)
    for e in range(nt):
        c = tp_from[e]
        for d in range(1, nk):
            block = res.at[kv_from[d], c]
            copy_to(block, block, rk_ss.at[e, d], rk_rs.at[e, d], "kv", kv_to[d]).wait_recv()
        at = pl.ds(pl.multiple_of(c * cols, 128), cols)
        part = res[:, c].astype(F32).reshape(tokens, cols)
        square = square + jnp.sum(part * part, axis=1, keepdims=True)
        x = (part * gain[:, at]).astype(BF16)
        for load, weight, acc in ((3, gate_w, acc_gate), (4, up_w, acc_up)):
            if e == 0:
                loaded(load)
            product = lax.dot_general(
                x, weight[:, at], (((1,), (1,)), ((), ())), preferred_element_type=F32
            )
            acc[...] = product if e == 0 else acc[...] + product
    inverse = lax.rsqrt(square / width + EPSILON)
    gate = acc_gate[...] * inverse
    hidden = (gate / (1.0 + jnp.exp(-gate)) * (acc_up[...] * inverse)).astype(BF16)
    loaded(5)

    half = nk // 2
    odd = lax.rem(k_me, 2)
    m_me = k_me // 2
    partner = k_me + 1 - 2 * odd
    m_to = [lax.rem(m_me + d, half) for d in range(half)]
    chunk = width // parts

    def to_partner(c):
        return copy_to(
            s_send.at[c, 1 - odd], s_recv.at[c], s_ss.at[c], s_rs.at[c], "kv", partner
        )

    def to_others(c, d):
        return copy_to(
            g_send.at[c, m_to[d]],
            g_recv.at[c, d],
            g_ss.at[c, d],
            g_rs.at[c, d],
            "kv",
            2 * m_to[d] + odd,
        )

    for c in range(parts + 1):
        if c < parts:
            product = jnp.dot(
                hidden, down_w[:, c * chunk : (c + 1) * chunk], preferred_element_type=F32
            ).reshape(half, 2, group, chunk)
            s_send[c, 0] = product[:, 0].astype(BF16)
            s_send[c, 1] = product[:, 1].astype(BF16)
            copy = to_partner(c)
            copy.start()
            sends.append(copy)
        if c > 0:
            to_partner(c - 1).wait_recv()
            g_send[c - 1] = (s_send[c - 1, odd].astype(F32) + s_recv[c - 1].astype(F32)).astype(
                BF16
            )
            for d in range(1, half):
                copy = to_others(c - 1, d)
                copy.start()
                sends.append(copy)

    row = lax.broadcasted_iota(jnp.int32, (group, cols), 0)
    for c in range(parts):
        mixed = g_send[c, m_me].astype(F32)
        for d in range(1, half):
            to_others(c, d).wait_recv()
            mixed = mixed + g_recv[c, d].astype(F32)
        for t in range(nt):
            f_send[c, t] = mixed[t * rows_own : (t + 1) * rows_own].astype(BF16)
        for d in range(1, nt):
            send(
                f_send.at[c, tp_to[d]],
                f_recv.at[c, d],
                f_ss.at[c, d],
                f_rs.at[c, d],
                "tp",
                tp_to[d],
            )
        for b in range(chunk // cols):
            first = c * (chunk // cols) + b
            here = mixed[:, b * cols : (b + 1) * cols] + res[k_me, first].astype(F32)
            for i in range(rows_own):
                own[i : i + 1, first * cols : (first + 1) * cols] = jnp.sum(
                    jnp.where(row == t_me * rows_own + i, here, 0.0), axis=0, keepdims=True
                )
    for c in range(parts):
        at = slice(c * chunk, (c + 1) * chunk)
        total = own[:, at]
        for d in range(1, nt):
            copy_to(
                f_send.at[c, tp_to[d]],
                f_recv.at[c, d],
                f_ss.at[c, d],
                f_rs.at[c, d],
                "tp",
                tp_to[d],
            ).wait_recv()
            total = total + f_recv[c, d].astype(F32)
        result[:, at] = total.astype(BF16)
    for copy in sends:
        copy.wait_send()


def hand_over(source, target, sem):
    copy = pltpu.make_async_copy(source, target, sem)
    copy.start()
    copy.wait()


def local(
    nk,
    nt,
    activations,
    queries,
    tree_cache_keys,
    tree_cache_values,
    parents,
    node_lengths,
    token_leaf,
    out_weight,
    norm_gain,
    gate_weight,
    up_weight,
    down_weight,
):
    group, q_width = queries.shape
    rows_own, width = activations.shape
    tokens = nk * group
    cols = width // nt
    units = gate_weight.shape[1]
    parts = 4
    chunk = width // parts
    dma = pltpu.SemaphoreType.DMA
    vmem = pl.BlockSpec(memory_space=pltpu.VMEM)
    smem = pl.BlockSpec(memory_space=pltpu.SMEM)
    anywhere = pl.BlockSpec(memory_space=pl.ANY)
    output = pl.pallas_call(
        functools.partial(layer_kernel, nk, nt, parts),
        out_shape=jax.ShapeDtypeStruct((rows_own, width), BF16),
        in_specs=[smem, smem, vmem, vmem, vmem, vmem] + [anywhere] * 6,
        out_specs=vmem,
        scratch_shapes=[
            pltpu.VMEM(tree_cache_keys.shape, BF16),
            pltpu.VMEM(tree_cache_values.shape, BF16),
            pltpu.VMEM(out_weight.shape, BF16),
            pltpu.VMEM((units, width), BF16),
            pltpu.VMEM((units, width), BF16),
            pltpu.VMEM(down_weight.shape, BF16),
            pltpu.VMEM((nk, group, q_width), BF16),
            pltpu.VMEM((nt, rows_own, width), F32),
            pltpu.VMEM((nk, group, q_width), BF16),
            pltpu.VMEM((nk, group, q_width), BF16),
            pltpu.VMEM((nk, 2, group, HEAD_WIDTH), F32),
            pltpu.VMEM((nk, 2, group, HEAD_WIDTH), F32),
            pltpu.VMEM((nt, group, cols), BF16),
            pltpu.VMEM((nt, group, cols), BF16),
            pltpu.VMEM((nk, nt, group, cols), BF16),
            pltpu.VMEM((tokens, units), F32),
            pltpu.VMEM((tokens, units), F32),
            pltpu.VMEM((parts, 2, nk // 2, group, chunk), BF16),
            pltpu.VMEM((parts, nk // 2, group, chunk), BF16),
            pltpu.VMEM((parts, nk // 2, group, chunk), BF16),
            pltpu.VMEM((parts, nk // 2, group, chunk), BF16),
            pltpu.VMEM((parts, nt, rows_own, chunk), BF16),
            pltpu.VMEM((parts, nt, rows_own, chunk), BF16),
            pltpu.VMEM((rows_own, width), F32),
            dma((6, LOAD_PIECES)),
            dma((nk,)),
            dma((nk,)),
            dma((nt,)),
            dma((nt,)),
            dma((nk,)),
            dma((nk,)),
            dma((nk,)),
            dma((nk,)),
            dma((nt,)),
            dma((nt,)),
            dma((nt,)),
            dma((nt,)),
            dma((nt, nk)),
            dma((nt, nk)),
            dma((parts,)),
            dma((parts,)),
            dma((parts, nk // 2)),
            dma((parts, nk // 2)),
            dma((parts, nt)),
            dma((parts, nt)),
        ],
        compiler_params=pltpu.CompilerParams(
            collective_id=0, has_side_effects=True, vmem_limit_bytes=58 * 2**20
        ),
        name="layer",
    )(
        parents,
        node_lengths,
        token_leaf.reshape(1, tokens),
        activations,
        queries,
        norm_gain.reshape(1, width),
        tree_cache_keys,
        tree_cache_values,
        out_weight,
        gate_weight.T,
        up_weight.T,
        down_weight,
    )
    return pl.pallas_call(
        hand_over,
        out_shape=jax.ShapeDtypeStruct(output.shape, BF16),
        in_specs=[pl.BlockSpec(memory_space=pltpu.HBM)],
        out_specs=pl.BlockSpec(memory_space=pltpu.HBM),
        scratch_shapes=[dma],
        name="hand_over",
    )(output)


def solution(mesh):
    return jax.shard_map(
        functools.partial(local, mesh.shape["kv"], mesh.shape["tp"]),
        mesh=mesh,
        in_specs=(
            P(("kv", "tp"), None),
            P("kv", "tp"),
            P("kv", "tp"),
            P("kv", "tp"),
            P(),
            P(),
            P(),
            P("tp", None),
            P(),
            P(None, ("kv", "tp")),
            P(None, ("kv", "tp")),
            P(("kv", "tp"), None),
        ),
        out_specs=P(("kv", "tp"), None),
        check_vma=False,
    )
```

```python
import functools
import math

import jax
import jax.numpy as jnp
from jax import lax
from jax.experimental import pallas as pl
from jax.experimental.pallas import tpu as pltpu
from jax.sharding import PartitionSpec as P

QUERY_HEADS = 40
KEY_VALUE_HEADS = 8
HEAD_WIDTH = 128
LOWEST = -1e30
EPSILON = 1e-06
MESH = pl.DeviceIdType.MESH
F32 = jnp.float32
BF16 = jnp.bfloat16
LOAD_PIECES = 2


def copy_to(source, target, send, receive, axis, peer):
    return pltpu.make_async_remote_copy(
        src_ref=source,
        dst_ref=target,
        send_sem=send,
        recv_sem=receive,
        device_id={axis: peer},
        device_id_type=MESH,
    )


def layer_kernel(
    nk,
    nt,
    parts,
    parents,
    lengths,
    leaf_row,
    act,
    query,
    gain,
    keys_hbm,
    values_hbm,
    out_hbm,
    gate_hbm,
    up_hbm,
    down_hbm,
    result,
    keys,
    values,
    out_w,
    gate_w,
    up_w,
    down_w,
    q_all,
    act_all,
    w_send,
    w_recv,
    ml_send,
    ml_recv,
    p_send,
    p_recv,
    res,
    acc_gate,
    acc_up,
    s_send,
    s_recv,
    g_send,
    g_recv,
    f_send,
    f_recv,
    own,
    load_sem,
    q_ss,
    q_rs,
    a_ss,
    a_rs,
    w_ss,
    w_rs,
    ml_ss,
    ml_rs,
    p_ss,
    p_rs,
    rt_ss,
    rt_rs,
    rk_ss,
    rk_rs,
    s_ss,
    s_rs,
    g_ss,
    g_rs,
    f_ss,
    f_rs,
):
    k_me = lax.axis_index("kv")
    t_me = lax.axis_index("tp")
    group, q_width = query.shape
    tokens = nk * group
    slots = keys.shape[0]
    kv_local = keys.shape[1] // HEAD_WIDTH
    per_kv = QUERY_HEADS // KEY_VALUE_HEADS
    width = act.shape[1]
    rows_own = act.shape[0]
    cols = width // nt

    loads = []
    for source, target in (
        (keys_hbm, keys),
        (values_hbm, values),
        (out_hbm, out_w),
        (gate_hbm, gate_w),
        (up_hbm, up_w),
        (down_hbm, down_w),
    ):
        rows = source.shape[0]
        pieces = LOAD_PIECES if rows % (LOAD_PIECES * 16) == 0 else 1
        size = rows // pieces
        loads.append(
            [
                pltpu.make_async_copy(
                    source.at[pl.ds(i * size, size)],
                    target.at[pl.ds(i * size, size)],
                    load_sem.at[len(loads), i],
                )
                for i in range(pieces)
            ]
        )

    def start(which):
        for copy in loads[which]:
            copy.start()

    def loaded(which):
        for copy in loads[which]:
            copy.wait()

    for which in range(3):
        start(which)

    q_all[k_me] = query[...]
    act_all[t_me] = act[...].astype(F32)

    barrier = pltpu.get_barrier_semaphore()
    for d in range(1, nk):
        pl.semaphore_signal(
            barrier, inc=1, device_id={"kv": lax.rem(k_me + d, nk)}, device_id_type=MESH
        )
    for d in range(1, nt):
        pl.semaphore_signal(
            barrier, inc=1, device_id={"tp": lax.rem(t_me + d, nt)}, device_id_type=MESH
        )
    pl.semaphore_wait(barrier, nk + nt - 2)

    kv_to = [lax.rem(k_me + d, nk) for d in range(nk)]
    kv_from = [lax.rem(k_me + nk - d, nk) for d in range(nk)]
    tp_to = [lax.rem(t_me + d, nt) for d in range(nt)]
    tp_from = [lax.rem(t_me + nt - d, nt) for d in range(nt)]
    sends = []

    def send(*args):
        copy = copy_to(*args)
        copy.start()
        sends.append(copy)

    for d in range(1, nk):
        send(q_all.at[k_me], q_all.at[k_me], q_ss.at[d], q_rs.at[d], "kv", kv_to[d])
    for d in range(1, nt):
        send(act_all.at[t_me], act_all.at[t_me], a_ss.at[d], a_rs.at[d], "tp", tp_to[d])

    slot_id = k_me * slots + lax.broadcasted_iota(jnp.int32, (1, slots), 1)
    node = jnp.zeros((1, slots), jnp.int32)
    end = jnp.int32(0)
    nodes = parents.shape[0]
    for n in range(nodes):
        end = end + lengths[n]
        node = node + jnp.where(slot_id >= end, 1, 0)
    node = jnp.where(node == nodes, -1, node)
    diagonal = lax.broadcasted_iota(jnp.int32, (tokens, tokens), 0) == lax.broadcasted_iota(
        jnp.int32, (tokens, tokens), 1
    )
    leaf = jnp.sum(
        jnp.where(diagonal, jnp.broadcast_to(leaf_row[...], (tokens, tokens)), 0),
        axis=1,
        keepdims=True,
    )
    tenant = jnp.zeros_like(leaf)
    for n in range(nodes):
        tenant = tenant + jnp.where(leaf == n, parents[n], 0)
    bias = jnp.where((node == 0) | (node == tenant) | (node == leaf), 0.0, LOWEST)[None]

    loaded(0)
    loaded(1)
    for d in range(1, nk):
        block = q_all.at[kv_from[d]]
        copy_to(block, block, q_ss.at[d], q_rs.at[d], "kv", kv_to[d]).wait_recv()

    for which in range(3, 6):
        start(which)

    lane = lax.broadcasted_iota(jnp.int32, (tokens, HEAD_WIDTH), 1)
    tops = jnp.zeros((tokens, HEAD_WIDTH), F32)
    sums = jnp.ones((tokens, HEAD_WIDTH), F32)
    for j in range(kv_local):
        stacked = jnp.concatenate(
            [
                q_all[:, :, h * HEAD_WIDTH : (h + 1) * HEAD_WIDTH]
                .astype(F32)
                .reshape(tokens, HEAD_WIDTH)
                for h in range(j * per_kv, (j + 1) * per_kv)
            ],
            axis=0,
        ).astype(BF16)
        head = slice(j * HEAD_WIDTH, (j + 1) * HEAD_WIDTH)
        scores = lax.dot_general(
            stacked, keys[:, head], (((1,), (1,)), ((), ())), preferred_element_type=F32
        ) * (1.0 / math.sqrt(HEAD_WIDTH))
        scores = scores.reshape(per_kv, tokens, slots) + bias
        top = jnp.max(scores, axis=2, keepdims=True)
        weights = jnp.exp(scores - top)
        total = jnp.sum(weights, axis=2, keepdims=True)
        weighted = jnp.dot(
            weights.astype(BF16).reshape(per_kv * tokens, slots),
            values[:, head],
            preferred_element_type=F32,
        ).reshape(per_kv, nk, group, HEAD_WIDTH)
        for g in range(per_kv):
            h = j * per_kv + g
            w_send[:, :, h * HEAD_WIDTH : (h + 1) * HEAD_WIDTH] = weighted[g].astype(BF16)
            tops = jnp.where(lane == h, top[g], tops)
            sums = jnp.where(lane == h, total[g], sums)
    ml_send[:, 0] = tops.reshape(nk, group, HEAD_WIDTH)
    ml_send[:, 1] = sums.reshape(nk, group, HEAD_WIDTH)

    for d in range(1, nk):
        send(ml_send.at[kv_to[d]], ml_recv.at[d], ml_ss.at[d], ml_rs.at[d], "kv", kv_to[d])
        send(w_send.at[kv_to[d]], w_recv.at[d], w_ss.at[d], w_rs.at[d], "kv", kv_to[d])
    ml_recv[0] = ml_send[k_me]
    w_recv[0] = w_send[k_me]
    loaded(2)
    for d in range(1, nk):
        copy_to(
            ml_send.at[kv_to[d]], ml_recv.at[d], ml_ss.at[d], ml_rs.at[d], "kv", kv_to[d]
        ).wait_recv()
        copy_to(
            w_send.at[kv_to[d]], w_recv.at[d], w_ss.at[d], w_rs.at[d], "kv", kv_to[d]
        ).wait_recv()
    highest = ml_recv[0, 0]
    for d in range(1, nk):
        highest = jnp.maximum(highest, ml_recv[d, 0])
    scales = [jnp.exp(ml_recv[d, 0] - highest) for d in range(nk)]
    denominator = scales[0] * ml_recv[0, 1]
    for d in range(1, nk):
        denominator = denominator + scales[d] * ml_recv[d, 1]
    pieces = []
    for h in range(kv_local * per_kv):
        total = jnp.zeros((group, HEAD_WIDTH), F32)
        for d in range(nk):
            part = w_recv[d, :, h * HEAD_WIDTH : (h + 1) * HEAD_WIDTH].astype(F32)
            total = total + part * scales[d][:, h : h + 1]
        pieces.append(total / denominator[:, h : h + 1])
    context = jnp.concatenate(pieces, axis=1).astype(BF16)

    for d in list(range(1, nt)) + [0]:
        at = pl.multiple_of(tp_to[d] * cols, 128)
        product = jnp.dot(context, out_w[:, pl.ds(at, cols)], preferred_element_type=F32)
        if d > 0:
            p_send[d] = product.astype(BF16)
            send(p_send.at[d], p_recv.at[d], p_ss.at[d], p_rs.at[d], "tp", tp_to[d])
    for d in range(1, nt):
        block = act_all.at[tp_from[d]]
        copy_to(block, block, a_ss.at[d], a_rs.at[d], "tp", tp_to[d]).wait_recv()
    mine = pl.ds(pl.multiple_of(t_me * cols, 128), cols)
    row = lax.broadcasted_iota(jnp.int32, (group, cols), 0)
    before = jnp.zeros((group, cols), F32)
    for t in range(nt):
        block = act_all[t, :, mine]
        for i in range(rows_own):
            before = jnp.where(
                row == t * rows_own + i, jnp.broadcast_to(block[i : i + 1], (group, cols)), before
            )
    attended = product
    for d in range(1, nt):
        copy_to(
            p_send.at[d], p_recv.at[d], p_ss.at[d], p_rs.at[d], "tp", tp_to[d]
        ).wait_recv()
        attended = attended + p_recv[d].astype(F32)
    res[k_me, t_me] = (before + attended).astype(BF16)

    block = res.at[k_me, t_me]
    for d in range(1, nt):
        send(block, block, rt_ss.at[d], rt_rs.at[d], "tp", tp_to[d])
    for e in range(nt):
        block = res.at[k_me, tp_from[e]]
        if e > 0:
            copy_to(block, block, rt_ss.at[e], rt_rs.at[e], "tp", tp_to[e]).wait_recv()
        for d in range(1, nk):
            send(block, block, rk_ss.at[e, d], rk_rs.at[e, d], "kv", kv_to[d])

    square = jnp.zeros((tokens, 1), F32)
    for e in range(nt):
        c = tp_from[e]
        for d in range(1, nk):
            block = res.at[kv_from[d], c]
            copy_to(block, block, rk_ss.at[e, d], rk_rs.at[e, d], "kv", kv_to[d]).wait_recv()
        at = pl.ds(pl.multiple_of(c * cols, 128), cols)
        part = res[:, c].astype(F32).reshape(tokens, cols)
        square = square + jnp.sum(part * part, axis=1, keepdims=True)
        x = (part * gain[:, at]).astype(BF16)
        for load, weight, acc in ((3, gate_w, acc_gate), (4, up_w, acc_up)):
            if e == 0:
                loaded(load)
            product = lax.dot_general(
                x, weight[:, at], (((1,), (1,)), ((), ())), preferred_element_type=F32
            )
            acc[...] = product if e == 0 else acc[...] + product
    inverse = lax.rsqrt(square / width + EPSILON)
    gate = acc_gate[...] * inverse
    hidden = (gate / (1.0 + jnp.exp(-gate)) * (acc_up[...] * inverse)).astype(BF16)
    loaded(5)

    half = nk // 2
    odd = lax.rem(k_me, 2)
    m_me = k_me // 2
    partner = k_me + 1 - 2 * odd
    m_to = [lax.rem(m_me + d, half) for d in range(half)]
    chunk = width // parts

    def to_partner(c):
        return copy_to(
            s_send.at[c, 1 - odd], s_recv.at[c], s_ss.at[c], s_rs.at[c], "kv", partner
        )

    def to_others(c, d):
        return copy_to(
            g_send.at[c, m_to[d]],
            g_recv.at[c, d],
            g_ss.at[c, d],
            g_rs.at[c, d],
            "kv",
            2 * m_to[d] + odd,
        )

    for c in range(parts + 1):
        if c < parts:
            product = jnp.dot(
                hidden, down_w[:, c * chunk : (c + 1) * chunk], preferred_element_type=F32
            ).reshape(half, 2, group, chunk)
            s_send[c, 0] = product[:, 0].astype(BF16)
            s_send[c, 1] = product[:, 1].astype(BF16)
            copy = to_partner(c)
            copy.start()
            sends.append(copy)
        if c > 0:
            to_partner(c - 1).wait_recv()
            g_send[c - 1] = (s_send[c - 1, odd].astype(F32) + s_recv[c - 1].astype(F32)).astype(
                BF16
            )
            for d in range(1, half):
                copy = to_others(c - 1, d)
                copy.start()
                sends.append(copy)

    row = lax.broadcasted_iota(jnp.int32, (group, cols), 0)
    for c in range(parts):
        mixed = g_send[c, m_me].astype(F32)
        for d in range(1, half):
            to_others(c, d).wait_recv()
            mixed = mixed + g_recv[c, d].astype(F32)
        for t in range(nt):
            f_send[c, t] = mixed[t * rows_own : (t + 1) * rows_own].astype(BF16)
        for d in range(1, nt):
            send(
                f_send.at[c, tp_to[d]],
                f_recv.at[c, d],
                f_ss.at[c, d],
                f_rs.at[c, d],
                "tp",
                tp_to[d],
            )
        for b in range(chunk // cols):
            first = c * (chunk // cols) + b
            here = mixed[:, b * cols : (b + 1) * cols] + res[k_me, first].astype(F32)
            for i in range(rows_own):
                own[i : i + 1, first * cols : (first + 1) * cols] = jnp.sum(
                    jnp.where(row == t_me * rows_own + i, here, 0.0), axis=0, keepdims=True
                )
    for c in range(parts):
        at = slice(c * chunk, (c + 1) * chunk)
        total = own[:, at]
        for d in range(1, nt):
            copy_to(
                f_send.at[c, tp_to[d]],
                f_recv.at[c, d],
                f_ss.at[c, d],
                f_rs.at[c, d],
                "tp",
                tp_to[d],
            ).wait_recv()
            total = total + f_recv[c, d].astype(F32)
        result[:, at] = total
    for copy in sends:
        copy.wait_send()


def local(
    nk,
    nt,
    activations,
    queries,
    tree_cache_keys,
    tree_cache_values,
    parents,
    node_lengths,
    token_leaf,
    out_weight,
    norm_gain,
    gate_weight,
    up_weight,
    down_weight,
):
    group, q_width = queries.shape
    rows_own, width = activations.shape
    tokens = nk * group
    cols = width // nt
    units = gate_weight.shape[1]
    parts = 2
    chunk = width // parts
    dma = pltpu.SemaphoreType.DMA
    vmem = pl.BlockSpec(memory_space=pltpu.VMEM)
    smem = pl.BlockSpec(memory_space=pltpu.SMEM)
    anywhere = pl.BlockSpec(memory_space=pl.ANY)
    output = pl.pallas_call(
        functools.partial(layer_kernel, nk, nt, parts),
        out_shape=jax.ShapeDtypeStruct((rows_own, width), F32),
        in_specs=[smem, smem, vmem, vmem, vmem, vmem] + [anywhere] * 6,
        out_specs=vmem,
        scratch_shapes=[
            pltpu.VMEM(tree_cache_keys.shape, BF16),
            pltpu.VMEM(tree_cache_values.shape, BF16),
            pltpu.VMEM(out_weight.shape, BF16),
            pltpu.VMEM((units, width), BF16),
            pltpu.VMEM((units, width), BF16),
            pltpu.VMEM(down_weight.shape, BF16),
            pltpu.VMEM((nk, group, q_width), BF16),
            pltpu.VMEM((nt, rows_own, width), F32),
            pltpu.VMEM((nk, group, q_width), BF16),
            pltpu.VMEM((nk, group, q_width), BF16),
            pltpu.VMEM((nk, 2, group, HEAD_WIDTH), F32),
            pltpu.VMEM((nk, 2, group, HEAD_WIDTH), F32),
            pltpu.VMEM((nt, group, cols), BF16),
            pltpu.VMEM((nt, group, cols), BF16),
            pltpu.VMEM((nk, nt, group, cols), BF16),
            pltpu.VMEM((tokens, units), F32),
            pltpu.VMEM((tokens, units), F32),
            pltpu.VMEM((parts, 2, nk // 2, group, chunk), BF16),
            pltpu.VMEM((parts, nk // 2, group, chunk), BF16),
            pltpu.VMEM((parts, nk // 2, group, chunk), BF16),
            pltpu.VMEM((parts, nk // 2, group, chunk), BF16),
            pltpu.VMEM((parts, nt, rows_own, chunk), BF16),
            pltpu.VMEM((parts, nt, rows_own, chunk), BF16),
            pltpu.VMEM((rows_own, width), F32),
            dma((6, LOAD_PIECES)),
            dma((nk,)),
            dma((nk,)),
            dma((nt,)),
            dma((nt,)),
            dma((nk,)),
            dma((nk,)),
            dma((nk,)),
            dma((nk,)),
            dma((nt,)),
            dma((nt,)),
            dma((nt,)),
            dma((nt,)),
            dma((nt, nk)),
            dma((nt, nk)),
            dma((parts,)),
            dma((parts,)),
            dma((parts, nk // 2)),
            dma((parts, nk // 2)),
            dma((parts, nt)),
            dma((parts, nt)),
        ],
        compiler_params=pltpu.CompilerParams(
            collective_id=0, has_side_effects=True, vmem_limit_bytes=58 * 2**20
        ),
        name="layer",
    )(
        parents,
        node_lengths,
        token_leaf.reshape(1, tokens),
        activations,
        queries,
        norm_gain.reshape(1, width),
        tree_cache_keys,
        tree_cache_values,
        out_weight,
        gate_weight.T,
        up_weight.T,
        down_weight,
    )
    return output.astype(BF16)


def solution(mesh):
    return jax.shard_map(
        functools.partial(local, mesh.shape["kv"], mesh.shape["tp"]),
        mesh=mesh,
        in_specs=(
            P(("kv", "tp"), None),
            P("kv", "tp"),
            P("kv", "tp"),
            P("kv", "tp"),
            P(),
            P(),
            P(),
            P("tp", None),
            P(),
            P(None, ("kv", "tp")),
            P(None, ("kv", "tp")),
            P(("kv", "tp"), None),
        ),
        out_specs=P(("kv", "tp"), None),
        check_vma=False,
    )
```
